128 devices in a mesh: row: 8 (over y, core), col: 16 (over z, x).
Axes of the slice: x: 4, y: 4, z: 4, core: 2. Of those that a mesh axis runs over, the one named last changes fastest.
Arguments:
- jac_row: bfloat16 [8, 16, 16, 2, 64, 3, 576], P('row', 'col'), may hold values from -0.25 to 0.25
- jac_col: bfloat16 [8, 16, 16, 2, 64, 3, 576], P('row', 'col'), may hold values from -0.25 to 0.25
- point_inv: bfloat16 [8, 16, 16, 2, 64, 9], P('row', 'col'), as said below
- pair_counts: int32 [8, 16, 16, 2], P('row', 'col'), may hold values from 16 to 64, as said below
- camera_blocks: float32 [16, 576, 576], P('row'), as said below
- right_side: float32 [16, 576], P('row'), may hold values from -300 to 300
Outputs:
- pair_blocks: float32 [16, 16, 576, 576], P('row', 'col')
- diagonal_blocks: float32 [16, 576, 576], P('row')
- solution: float32 [16, 576], P('row')
- residual: float32 [16, 576], P('row')
The draws below stay inside these ranges and needn't reach their ends.
Inputs may be any that keep to these rules, and one draw needn't show every extreme that they name: `pair_counts`: one co-visibility list of every device holds 64 live tracks. `point_inv`: each 3 x 3 block is symmetric positive definite. `camera_blocks`: each block is symmetric; S and its diagonal blocks are positive definite.
All inputs are finite; a program needn't handle non-finite values.
Results may differ from the reference program's by a relative error of at most 0.0049.
Values may be sent and summed in bfloat16 or wider, within the bound.
A program may use at most 256 MiB of HBM per device.

```python
import math
import jax
import jax.numpy as jnp
from jax import lax

BLK = 576
SLOT = 64
ITERS = 2
GROUPS = 16
GR = 2
N_ROW = 8
N_COL = 16


def draw_point_inv(key, part):
    key = jax.random.fold_in(key, 7)
    first, second = jax.random.split(key)
    shape = (N_ROW, N_COL, GROUPS, GR, SLOT, 3)
    scales = jnp.exp(jax.random.uniform(first, shape, jnp.float32, math.log(0.3), math.log(2.4)))
    corr = jax.random.uniform(second, shape, jnp.float32, -0.3, 0.3)
    root = jnp.sqrt(scales)
    c01 = corr[..., 0] * root[..., 0] * root[..., 1]
    c02 = corr[..., 1] * root[..., 0] * root[..., 2]
    c12 = corr[..., 2] * root[..., 1] * root[..., 2]
    entries = jnp.stack([scales[..., 0], c01, c02, c01, scales[..., 1], c12, c02, c12, scales[..., 2]], axis=-1)
    return entries.astype(jnp.bfloat16)


def draw_pair_counts(key, part):
    key = jax.random.fold_in(key, 5)
    first, second = jax.random.split(key)
    shape = (N_ROW, N_COL, GROUPS, GR)
    lowest = max(1, SLOT // 4)
    counts = jax.random.randint(first, shape, lowest, SLOT + SLOT // 2 + 1)
    counts = jnp.minimum(counts, SLOT)
    chosen = jax.random.randint(second, (N_ROW, N_COL, 1, 1), 0, GROUPS * GR)
    position = jnp.arange(GROUPS * GR, dtype=jnp.int32).reshape(1, 1, GROUPS, GR)
    return jnp.where(position == chosen, SLOT, counts).astype(jnp.int32)


def draw_camera_blocks(key, part):
    key = jax.random.fold_in(key, 11)
    first, second = jax.random.split(key)
    shift = 1.5 * 2.0 * 3.0 * 1.35 * N_COL * GROUPS * SLOT / BLK
    diag = jnp.exp(jax.random.uniform(first, (GROUPS, BLK), jnp.float32, math.log(120.0), math.log(240.0)))
    diag = diag + shift
    noise = jax.random.uniform(second, (GROUPS, BLK, BLK), jnp.float32, -0.02, 0.02)
    sym = 0.5 * (noise + jnp.swapaxes(noise, 1, 2))
    eye = jnp.eye(BLK, dtype=jnp.float32)
    return sym * (1.0 - eye) + diag[:, :, None] * eye


def levels(rng, dims, shards, low, high):
    gain, own = 1.0, jax.random.fold_in(rng, 6)
    for dim, shards_of in shards:
        steps = jnp.exp(jax.random.uniform(jax.random.fold_in(own, dim), (shards_of,), jnp.float32, low / len(shards), high / len(shards)))
        gain = gain * jnp.repeat(steps, dims[dim] // shards_of).reshape([-1 if axis == dim else 1 for axis in range(len(dims))])
    return gain


def normal_values(stream_key, dims, scale, limit, pieces=(), held_as=jnp.bfloat16):
    result = jax.random.normal(stream_key, dims, jnp.float32) * scale
    if len(pieces) > 0:
        result = levels(stream_key, dims, pieces, -0.22, 0.18) * result
    return jnp.clip(result, min=-limit, max=limit).astype(held_as)


def setup_inputs(seed: int = 0) -> dict:
    key_of = jax.random.split(jax.random.key(seed), 7)
    return {
        "jac_row": normal_values(key_of[0], (N_ROW, N_COL, GROUPS, GR, SLOT, 3, BLK), BLK ** -0.5, 0.25, ((0, 8), (1, 16))),
        "jac_col": normal_values(key_of[1], (N_ROW, N_COL, GROUPS, GR, SLOT, 3, BLK), BLK ** -0.5, 0.25, ((0, 8), (1, 16))),
        "point_inv": draw_point_inv(jax.random.fold_in(key_of[6], 71), 0),
        "pair_counts": draw_pair_counts(jax.random.fold_in(key_of[6], 71), 0),
        "camera_blocks": draw_camera_blocks(jax.random.fold_in(key_of[6], 71), 0),
        "right_side": normal_values(key_of[5], (GROUPS, BLK), 50.0, 300.0, ((0, 8),), jnp.float32),
    }


def apply_inverse(inverse, jac):
    inv = inverse.astype(jnp.float32)
    wide = jac.astype(jnp.float32)
    rows = [inv[..., 3 * k, None] * wide[..., 0, :] + inv[..., 3 * k + 1, None] * wide[..., 1, :] + inv[..., 3 * k + 2, None] * wide[..., 2, :] for k in range(3)]
    return jnp.stack(rows, axis=-2).astype(jnp.bfloat16)

def solve_blocks(factor, vec):
    half = lax.linalg.triangular_solve(factor, vec[..., None], left_side=True, lower=True)
    whole = lax.linalg.triangular_solve(factor, half, left_side=True, lower=True, transpose_a=True)
    return whole[..., 0]

def reference(jac_row, jac_col, point_inv, pair_counts, camera_blocks, right_side):
    groups = jac_row.shape[2]
    slots = jac_row.shape[4]
    width = jac_row.shape[6]
    live = jnp.arange(slots, dtype=jnp.int32) < pair_counts[..., None]
    masked = point_inv * live[..., None].astype(jnp.bfloat16)

    def one_row(index):
        w_row = jac_row[index]
        w_col = jac_col[index]
        inverse = masked[index]
        row_img = apply_inverse(inverse, w_row).astype(jnp.float32)
        col_img = apply_inverse(inverse, w_col).astype(jnp.float32)
        wide_row = w_row.astype(jnp.float32)
        wide_col = w_col.astype(jnp.float32)
        own_row = jnp.einsum('cjaskp,cjaskq->apq', wide_row, row_img)
        pairs = jnp.einsum('cjaskp,cjaskq->ajpq', wide_row, col_img)
        own_col = jnp.einsum('cjaskp,cjaskq->jpq', wide_col, col_img)
        return (own_row, pairs, own_col)
    row_all, pair_all, col_all = lax.map(one_row, jnp.arange(N_ROW, dtype=jnp.int32))
    row_terms = row_all.reshape(groups, width, width)
    pair_blocks = pair_all.reshape(groups, groups, width, width)
    col_terms = jnp.sum(col_all, axis=0)
    diagonal = camera_blocks - row_terms - col_terms
    index = jnp.arange(groups, dtype=jnp.int32)
    self_pairs = pair_blocks[index, index]
    precond = diagonal - (self_pairs + jnp.swapaxes(self_pairs, 1, 2))
    factor = jnp.linalg.cholesky(precond)
    high = lax.Precision.HIGHEST

    def product(vec):
        own = jnp.einsum('gpq,gq->gp', diagonal, vec, precision=high)
        forward = jnp.einsum('ijpq,jq->ip', pair_blocks, vec, precision=high)
        backward = jnp.einsum('ijpq,ip->jq', pair_blocks, vec, precision=high)
        return own - forward - backward
    solution = jnp.zeros_like(right_side)
    residual = right_side
    pre_res = solve_blocks(factor, residual)
    direction = pre_res
    rz_now = jnp.sum(residual * pre_res)
    for step in range(ITERS):
        image = product(direction)
        alpha = rz_now / jnp.sum(direction * image)
        solution = solution + alpha * direction
        residual = residual - alpha * image
        if step + 1 < ITERS:
            pre_res = solve_blocks(factor, residual)
            rz_next = jnp.sum(residual * pre_res)
            direction = pre_res + rz_next / rz_now * direction
            rz_now = rz_next
    return (pair_blocks, diagonal, solution, residual)
```

```python
import functools
import jax
import jax.numpy as jnp
from jax import lax
from jax.experimental import pallas as pl
from jax.experimental.pallas import tpu as pltpu
from jax.sharding import PartitionSpec as P

MESH = pl.DeviceIdType.MESH
F32 = jnp.float32
BF16 = jnp.bfloat16
NROW, NCOL, GR, SLOT, BLK = 8, 16, 2, 64, 576
K3 = 3 * SLOT
CH = 72
ITERS = 2


def tn(lhs, rhs):
    return lax.dot_general(lhs, rhs, (((0,), (0,)), ((), ())), preferred_element_type=F32)


def form_kernel(minv, wrow, wcol, cam, tile, dchunk, pg_out,
                rmin, rrow, rcol, ownr, ownc, big, srow, qrow, scol, qcol, pg, camv,
                send_sem, recv_sem, loc_sem, rs_send, rs_recv, cs_send, cs_recv, pg_send, pg_recv):
    r = lax.axis_index("row")
    c = lax.axis_index("col")
    cg = c // GR
    half = c // NROW
    g = GR * r + half
    part = c % NROW

    def col_dst(i):
        return cg, (c % GR) * NROW + i

    barrier = pltpu.get_barrier_semaphore()

    def greet_row(d, n):
        pl.semaphore_signal(barrier, inc=1, device_id=(r, lax.rem(c + d, NCOL)), device_id_type=MESH)
        return n
    lax.fori_loop(1, NCOL, greet_row, 0)

    def greet_col(i, n):
        other = jnp.logical_or(i != r, g != c)

        @pl.when(other)
        def _():
            pl.semaphore_signal(barrier, inc=1, device_id=(i, g), device_id_type=MESH)
        return n
    lax.fori_loop(0, NROW, greet_col, 0)
    own_dst = jnp.logical_and(r == cg, c // NROW == c % GR)
    pl.semaphore_wait(barrier, NCOL - 1 + NROW - own_dst.astype(jnp.int32))

    def copies(d):
        j = lax.rem(c + d, NCOL)
        dev = (r, j)
        return [pltpu.make_async_remote_copy(src_ref=src.at[j], dst_ref=dst.at[d], send_sem=send_sem.at[n, d],
                                             recv_sem=recv_sem.at[n, d], device_id=dev, device_id_type=MESH)
                for n, (src, dst) in enumerate(((minv, rmin), (wcol, rcol), (wrow, rrow)))]

    def locals_():
        return [pltpu.make_async_copy(src.at[c], dst.at[0], loc_sem.at[n])
                for n, (src, dst) in enumerate(((minv, rmin), (wcol, rcol), (wrow, rrow)))] + [
            pltpu.make_async_copy(cam.at[c], camv, loc_sem.at[3])]

    for cp in locals_():
        cp.start()

    def start(d, n):
        for cp in copies(d):
            cp.start()
        return n
    lax.fori_loop(1, NCOL, start, 0)

    tile[...] = jnp.zeros_like(tile)
    ownr[...] = jnp.zeros_like(ownr)
    ownc[...] = jnp.zeros_like(ownc)

    row_i = lax.broadcasted_iota(jnp.int32, (SLOT, K3), 0)
    col_i = lax.broadcasted_iota(jnp.int32, (SLOT, K3), 1)
    eye = jnp.where(lax.rem(col_i, SLOT) == row_i, 1.0, 0.0).astype(F32)

    def chunk(d):
        for a in range(GR):
            ent = rmin[d, 8 * a:8 * a + 8, :].astype(F32)
            for k in range(3):
                big[SLOT * k:SLOT * (k + 1), :] = (eye * ent[k:k + 1, :]).astype(BF16)
            wr = rrow[d, K3 * a:K3 * (a + 1), :]
            wc = rcol[d, K3 * a:K3 * (a + 1), :]
            ci = jnp.dot(big[...], wc, preferred_element_type=F32).astype(BF16)
            ri = jnp.dot(big[...], wr, preferred_element_type=F32).astype(BF16)
            for lo, hi in ((0, 256), (256, 512), (512, 576)):
                tile[a, lo:hi, :] += tn(wr[:, lo:hi], ci)
                ownr[a, lo:hi, :] += tn(wr[:, lo:hi], ri)
                ownc[lo:hi, :] += tn(wc[:, lo:hi], ci)

    for cp in locals_()[:3]:
        cp.wait()
    chunk(0)

    def step(d, n):
        for cp in copies(d):
            cp.wait_recv()
        chunk(d)
        return n
    lax.fori_loop(1, NCOL, step, 0)

    for m in range(NCOL):
        a, i = divmod(m, NROW)
        srow[m] = ownr[a, CH * i:CH * (i + 1), :].astype(BF16)
    for i in range(NROW):
        scol[i] = ownc[CH * i:CH * (i + 1), :].astype(BF16)

    def row_copy(d):
        j = lax.rem(c + d, NCOL)
        return pltpu.make_async_remote_copy(src_ref=srow.at[j], dst_ref=qrow.at[d], send_sem=rs_send.at[d],
                                            recv_sem=rs_recv.at[d], device_id=(r, j), device_id_type=MESH)

    def col_copy(i):
        return pltpu.make_async_remote_copy(src_ref=scol.at[i], dst_ref=qcol.at[r], send_sem=cs_send.at[i],
                                            recv_sem=cs_recv.at[r], device_id=col_dst(i), device_id_type=MESH)

    def stays(i):
        return jnp.logical_and(own_dst, i == part)

    def col_start(i, n):
        @pl.when(jnp.logical_not(stays(i)))
        def _():
            col_copy(i).start()

        @pl.when(stays(i))
        def _():
            qcol[r] = scol[i]
        return n
    lax.fori_loop(0, NROW, col_start, 0)

    def row_start(d, n):
        row_copy(d).start()
        return n
    lax.fori_loop(1, NCOL, row_start, 0)

    locals_()[3].wait()
    dchunk[...] = camv[...] - srow[c].astype(F32)

    def col_sum(i, n):
        @pl.when(jnp.logical_or(i != r, g != c))
        def _():
            pltpu.make_async_remote_copy(src_ref=scol.at[i], dst_ref=qcol.at[i], send_sem=cs_send.at[i],
                                         recv_sem=cs_recv.at[i], device_id=(i, g), device_id_type=MESH).wait_recv()
        dchunk[...] -= qcol[i].astype(F32)
        return n
    lax.fori_loop(0, NROW, col_sum, 0)

    def row_sum(d, n):
        row_copy(d).wait_recv()
        dchunk[...] -= qrow[d].astype(F32)
        return n
    lax.fori_loop(1, NCOL, row_sum, 0)

    is_p = cg == r

    def pg_copy(i):
        return pltpu.make_async_remote_copy(src_ref=dchunk, dst_ref=pg.at[i], send_sem=pg_send, recv_sem=pg_recv.at[i],
                                            device_id=(r, g), device_id_type=MESH)

    @pl.when(g != c)
    def _():
        pg_copy(part).start()

    def drain(d, n):
        for cp in copies(d):
            cp.wait_send()
        row_copy(d).wait_send()
        return n
    lax.fori_loop(1, NCOL, drain, 0)

    def drain_col(i, n):
        @pl.when(jnp.logical_not(stays(i)))
        def _():
            col_copy(i).wait_send()
        return n
    lax.fori_loop(0, NROW, drain_col, 0)

    @pl.when(g != c)
    def _():
        pg_copy(part).wait_send()

    def gather(i, n):
        src_c = (c % GR) * NROW + i

        @pl.when(jnp.logical_and(is_p, src_c != c))
        def _():
            pg_copy(i).wait_recv()
            pg_out[i] = pg[i]

        @pl.when(jnp.logical_and(is_p, src_c == c))
        def _():
            pg_out[i] = dchunk[...]

        @pl.when(jnp.logical_not(is_p))
        def _():
            rows = lax.broadcasted_iota(jnp.int32, (CH, BLK), 0) + i * CH
            cols = lax.broadcasted_iota(jnp.int32, (CH, BLK), 1)
            pg_out[i] = jnp.where(rows == cols, 1.0, 0.0).astype(F32)
        return n
    lax.fori_loop(0, NROW, gather, 0)


def form(minv, wrow, wcol, cam):
    any_ = pl.BlockSpec(memory_space=pl.ANY)
    vm = pl.BlockSpec(memory_space=pltpu.VMEM)
    dma = pltpu.SemaphoreType.DMA
    return pl.pallas_call(
        form_kernel,
        out_shape=(jax.ShapeDtypeStruct((GR, BLK, BLK), F32), jax.ShapeDtypeStruct((CH, BLK), F32),
                   jax.ShapeDtypeStruct((NROW, CH, BLK), F32)),
        in_specs=[any_] * 4,
        out_specs=(vm, vm, vm),
        scratch_shapes=[
            pltpu.VMEM((NCOL, 16, K3), BF16),
            pltpu.VMEM((NCOL, GR * K3, BLK), BF16),
            pltpu.VMEM((NCOL, GR * K3, BLK), BF16),
            pltpu.VMEM((GR, BLK, BLK), F32),
            pltpu.VMEM((BLK, BLK), F32),
            pltpu.VMEM((K3, K3), BF16),
            pltpu.VMEM((NCOL, CH, BLK), BF16),
            pltpu.VMEM((NCOL, CH, BLK), BF16),
            pltpu.VMEM((NROW, CH, BLK), BF16),
            pltpu.VMEM((NROW, CH, BLK), BF16),
            pltpu.VMEM((NROW, CH, BLK), F32),
            pltpu.VMEM((CH, BLK), F32),
            dma((3, NCOL)), dma((3, NCOL)), dma((4,)),
            dma((NCOL,)), dma((NCOL,)), dma((NROW,)), dma((NROW,)),
            dma, dma((NROW,)),
        ],
        compiler_params=pltpu.CompilerParams(collective_id=0, has_side_effects=True, vmem_limit_bytes=56 * 2**20),
        name="form",
    )(minv, wrow, wcol, cam)


def minv_table(point_inv, pair_counts):
    inv = point_inv.reshape(NCOL, GR, SLOT, 3, 3)
    live = lax.broadcasted_iota(jnp.int32, (NCOL, GR, SLOT), 2) < pair_counts.reshape(NCOL, GR)[:, :, None]
    masked = inv * live[..., None, None].astype(BF16)
    rows = jnp.transpose(masked, (0, 1, 3, 4, 2)).reshape(NCOL, GR, 3, K3)
    return jnp.pad(rows, ((0, 0), (0, 0), (0, 5), (0, 0))).reshape(NCOL, 16, K3)


def stack_rows(jac):
    return jnp.transpose(jac.reshape(jac.shape[2:]), (0, 1, 3, 2, 4)).reshape(NCOL, GR * K3, BLK)


def mm(lhs, rhs):
    return jnp.dot(lhs.astype(BF16), rhs.astype(BF16), preferred_element_type=F32)


def mm_high(lhs, rhs):
    return jnp.dot(lhs, rhs, preferred_element_type=F32, precision=lax.Precision.HIGHEST)


def inverse_kernel(pg, tile, xinv, pmat, pair, e, y, res, sem):
    r = lax.axis_index("row")
    c = lax.axis_index("col")
    is_p = (c // GR == r).astype(F32)
    cp = pltpu.make_async_copy(tile.at[c % GR], pair, sem)
    cp.start()
    rows = lax.broadcasted_iota(jnp.int32, (BLK, BLK), 0)
    cols = lax.broadcasted_iota(jnp.int32, (BLK, BLK), 1)
    eye = jnp.where(rows == cols, 1.0, 0.0).astype(F32)
    cp.wait()
    own = pair[...] * is_p
    p = pg[...] - own - own.T
    pmat[...] = p
    dd = p * eye
    s_row = lax.rsqrt(jnp.sum(dd, axis=0, keepdims=True))
    s_col = lax.rsqrt(jnp.sum(dd, axis=1, keepdims=True))
    b = p * s_row * s_col
    e[...] = eye - b
    e2 = mm(e[...], e[...])
    f2 = jnp.sum(e2 * e2)

    @pl.when(f2 < 0.9)
    def _():
        y[...] = e[...] + e2 + mm(e[...], e2)

    @pl.when(jnp.logical_not(f2 < 0.9))
    def _():
        big = jnp.max(jnp.sum(jnp.abs(eye - e[...]), axis=1, keepdims=True))
        y[...] = eye * (1.0 / big - 1.0)

    def residual(mul):
        out = e[...] - y[...] + mul(y[...], e[...])
        res[...] = out
        return jnp.sum(out * out)

    def more(state):
        step, size = state
        return jnp.logical_and(size > 1.6e-5, step < 64)

    def newton(state):
        step, _ = state

        def low():
            y[...] = y[...] + res[...] + mm(res[...], y[...])
            return residual(mm)

        def high():
            y[...] = y[...] + res[...] + mm_high(res[...], y[...])
            return residual(mm_high)
        return step + 1, lax.cond(step < 6, low, high)
    lax.while_loop(more, newton, (jnp.int32(0), residual(mm)))
    xinv[...] = (eye + y[...]) * s_row * s_col


def inverse(pg, tile):
    vm = pl.BlockSpec(memory_space=pltpu.VMEM)
    sq = jax.ShapeDtypeStruct((BLK, BLK), F32)
    return pl.pallas_call(
        inverse_kernel,
        out_shape=(sq, sq),
        in_specs=[vm, pl.BlockSpec(memory_space=pl.ANY)],
        out_specs=(vm, vm),
        scratch_shapes=[pltpu.VMEM((BLK, BLK), F32)] * 4 + [pltpu.SemaphoreType.DMA],
        compiler_params=pltpu.CompilerParams(vmem_limit_bytes=48 * 2**20),
        name="inverse",
    )(pg, tile)


LT = 5
REFINE = 2


def lanes(t):
    return 128 * t, min(128 * (t + 1), BLK)


def spread(mat, vec):
    rows = mat.shape[0]
    acc = jnp.zeros((rows, 128), F32)
    for t in range(LT):
        lo, hi = lanes(t)
        part = mat[:, lo:hi] * vec[t:t + 1, :hi - lo]
        if hi - lo < 128:
            part = jnp.concatenate([part, jnp.zeros((rows, 128 - (hi - lo)), F32)], axis=1)
        acc = acc + part
    return acc


def fold(acc):
    out = []
    for t in range(LT):
        lo, hi = lanes(t)
        blk = acc[lo:hi, :]
        if hi - lo < 128:
            blk = jnp.concatenate([blk, jnp.zeros((128 - (hi - lo), 128), F32)], axis=0)
        out.append(jnp.sum(blk.T, axis=0, keepdims=True))
    return jnp.concatenate(out + [jnp.zeros((8 - LT, 128), F32)], axis=0)


def columns(vec):
    return jnp.concatenate([jnp.broadcast_to(vec[t:t + 1, :], (128, 128)).T for t in range(LT)], axis=0)


def matvec(mat, vec):
    return fold(spread(mat, vec))


def cg_kernel(tile, dchunk, xinv, pmat, rhs, diag, sol, resid,
              zbuf, zsrc, cbuf, csrc, bbuf, bsrc, sbuf, ssrc, fbuf, fsrc, acc, state,
              g_loc, g_send, g_recv, zr_send, zc_send, z_recv, c_send, b_send, c_recv, b_recv,
              s_send, s_recv, f_send, f_recv):
    r = lax.axis_index("row")
    c = lax.axis_index("col")
    ap = c % GR
    cg = c // GR
    half = c // NROW
    part = c % NROW
    is_p = cg == r
    not_p = jnp.logical_not(is_p)

    barrier = pltpu.get_barrier_semaphore()

    def greet(i, n):
        pl.semaphore_signal(barrier, inc=1, device_id=(r, lax.rem(c + i, NCOL)), device_id_type=MESH)

        @pl.when(i < NROW)
        def _():
            pl.semaphore_signal(barrier, inc=1, device_id=(lax.rem(r + i, NROW), c), device_id_type=MESH)

        @pl.when(is_p)
        def _():
            other = lax.rem(c + i, NCOL)
            pl.semaphore_signal(barrier, inc=1, device_id=(other // GR, other), device_id_type=MESH)
        return n
    lax.fori_loop(1, NCOL, greet, 0)
    pl.semaphore_wait(barrier, NCOL - 1 + NROW - 1 + (NCOL - 1) * is_p.astype(jnp.int32))

    def rc(src, dst, ss, rs, dev):
        return pltpu.make_async_remote_copy(src_ref=src, dst_ref=dst, send_sem=ss, recv_sem=rs, device_id=dev,
                                            device_id_type=MESH)

    def each(lo, hi, fn):
        def body(i, n):
            fn(i)
            return n
        lax.fori_loop(lo, hi, body, 0)

    def g_copy(d):
        return rc(dchunk, diag.at[c], g_send.at[d], g_recv.at[d], (r, lax.rem(c + d, NCOL)))

    def g_from(d):
        return rc(dchunk, diag.at[lax.rem(c - d + NCOL, NCOL)], g_send.at[d], g_recv.at[d], (r, lax.rem(c + d, NCOL)))

    def zr_copy(it, d):
        return rc(zsrc.at[it], zbuf.at[it, ap], zr_send.at[it, d], z_recv.at[it, ap], (r, lax.rem(c + d, NCOL)))

    def zc_copy(it, d):
        return rc(zsrc.at[it], zbuf.at[it, 2], zc_send.at[it, d], z_recv.at[it, 2], (lax.rem(r + d, NROW), c))

    def z_from(it, slot):
        return rc(zsrc.at[it], zbuf.at[it, slot], zr_send.at[it, 0], z_recv.at[it, slot], (lax.rem(r + 1, NROW), c))

    def s_copy(it, k, d):
        other = lax.rem(c + d, NCOL)
        return rc(ssrc.at[it, k], sbuf.at[it, k, c], s_send.at[it, k, d], s_recv.at[it, k, c], (other // GR, other))

    def s_from(it, k, i):
        return rc(ssrc.at[it, k], sbuf.at[it, k, i], s_send.at[it, k, 0], s_recv.at[it, k, i], (i // GR, i))

    def c_copy(it, a):
        return rc(csrc.at[it, a], cbuf.at[it, c], c_send.at[it, a], c_recv.at[it, c], (r, GR * r + a))

    def c_from(it, i):
        return rc(csrc.at[it, 0], cbuf.at[it, i], c_send.at[it, 0], c_recv.at[it, i], (r, i))

    def b_copy(it):
        return rc(bsrc.at[it], bbuf.at[it, r], b_send.at[it], b_recv.at[it, r], (cg, c))

    def b_from(it, i):
        return rc(bsrc.at[it], bbuf.at[it, i], b_send.at[it], b_recv.at[it, i], (i, c))

    def f_copy(d):
        return rc(fsrc, fbuf.at[ap], f_send.at[d], f_recv.at[ap], (r, lax.rem(c + d, NCOL)))

    def f_from(a):
        return rc(fsrc, fbuf.at[a], f_send.at[0], f_recv.at[a], (r, GR * r + a))

    def total(it, k):
        def wait(i):
            @pl.when(i != c)
            def _():
                s_from(it, k, i).wait_recv()
        each(0, NCOL, wait)
        sbuf[it, k, c] = ssrc[it, k]
        return jnp.sum(sbuf[it, k], axis=0)

    X, RES, D, IM, RZ = range(5)

    def exchange(it, k, value):
        ssrc[it, k] = jnp.zeros((8, 128), F32) + jnp.sum(value)
        each(1, NCOL, lambda d: s_copy(it, k, d).start())

    @pl.when(is_p)
    def _():
        state[X] = jnp.zeros((8, 128), F32)
        state[RES] = rhs[ap]

    def solve(it):
        res = state[RES]
        z = matvec(xinv, res)
        for _ in range(REFINE):
            z = z + matvec(xinv, res - matvec(pmat, z))
        zsrc[it] = z
        each(1, NCOL, lambda d: zr_copy(it, d).start())
        each(1, NROW, lambda d: zc_copy(it, d).start())
        exchange(it, 0, res * z)
        zbuf[it, ap] = z
        zbuf[it, 2] = z

    for it in range(ITERS):
        @pl.when(is_p)
        def _():
            solve(it)
        if it == 0:
            cp = pltpu.make_async_copy(dchunk, diag.at[c], g_loc)
            cp.start()
            each(1, NCOL, lambda d: g_copy(d).start())

        for slot in range(3):
            @pl.when(not_p if slot == 2 else c != GR * r + slot)
            def _():
                z_from(it, slot).wait_recv()

        zc = zbuf[it, 2]
        back = [jnp.zeros((1, hi - lo), F32) for lo, hi in map(lanes, range(LT))]
        for a in range(GR):
            acc[a] = -spread(tile[a], zc)
            zcol = columns(zbuf[it, a])
            for t in range(LT):
                lo, hi = lanes(t)
                back[t] = back[t] + jnp.sum(tile[a, :, lo:hi] * zcol[:BLK, :hi - lo], axis=0, keepdims=True)
        rows = pl.ds(pl.multiple_of(part * CH, 8), CH)
        acc[half, rows, :] += spread(dchunk[...], zbuf[it, half])
        back[LT - 1] = jnp.concatenate([back[LT - 1], jnp.zeros((1, 128 * LT - BLK), F32)], axis=1)
        bsrc[it] = jnp.concatenate(back + [jnp.zeros((8 - LT, 128), F32)], axis=0)

        @pl.when(not_p)
        def _():
            b_copy(it).start()
        for a in range(GR):
            csrc[it, a] = fold(acc[a])

            @pl.when(c != GR * r + a)
            def _():
                c_copy(it, a).start()

        @pl.when(is_p)
        def _():
            cbuf[it, c] = csrc[it, ap]
            bbuf[it, r] = bsrc[it]

            def wait_c(i):
                @pl.when(i != c)
                def _():
                    c_from(it, i).wait_recv()

            def wait_b(i):
                @pl.when(i != r)
                def _():
                    b_from(it, i).wait_recv()
            rz = total(it, 0)
            each(0, NCOL, wait_c)
            each(0, NROW, wait_b)
            image = jnp.sum(cbuf[it], axis=0) - jnp.sum(bbuf[it], axis=0)
            direction = zsrc[it]
            if it > 0:
                beta = rz / state[RZ]
                direction = direction + beta * state[D]
                image = image + beta * state[IM]
            state[RZ] = rz
            state[D] = direction
            state[IM] = image
            exchange(it, 1, direction * image)
            alpha = rz / total(it, 1)
            state[X] = state[X] + alpha * direction
            state[RES] = state[RES] - alpha * image

    @pl.when(is_p)
    def _():
        fsrc[0] = state[X]
        fsrc[1] = state[RES]
        each(1, NCOL, lambda d: f_copy(d).start())
        fbuf[ap] = fsrc[...]

    for a in range(GR):
        @pl.when(c != GR * r + a)
        def _():
            f_from(a).wait_recv()
        sol[a] = fbuf[a, 0]
        resid[a] = fbuf[a, 1]

    pltpu.make_async_copy(dchunk, diag.at[c], g_loc).wait()
    each(1, NCOL, lambda d: g_from(d).wait_recv())
    each(1, NCOL, lambda d: g_copy(d).wait_send())
    for it in range(ITERS):
        @pl.when(not_p)
        def _():
            b_copy(it).wait_send()
        for a in range(GR):
            @pl.when(c != GR * r + a)
            def _():
                c_copy(it, a).wait_send()

    @pl.when(is_p)
    def _():
        for it in range(ITERS):
            each(1, NCOL, lambda d: zr_copy(it, d).wait_send())
            each(1, NROW, lambda d: zc_copy(it, d).wait_send())
            for k in range(2):
                each(1, NCOL, lambda d: s_copy(it, k, d).wait_send())
        each(1, NCOL, lambda d: f_copy(d).wait_send())


def gradients(tile, dchunk, xinv, pmat, rhs):
    vm = pl.BlockSpec(memory_space=pltpu.VMEM)
    dma = pltpu.SemaphoreType.DMA
    v = lambda *lead: pltpu.VMEM((*lead, 8, 128), F32)
    vec = jax.ShapeDtypeStruct((GR, 8, 128), F32)
    return pl.pallas_call(
        cg_kernel,
        out_shape=(jax.ShapeDtypeStruct((NCOL, CH, BLK), F32), vec, vec),
        in_specs=[vm] * 5,
        out_specs=(pl.BlockSpec(memory_space=pl.ANY), vm, vm),
        scratch_shapes=[
            v(ITERS, 3), v(ITERS), v(ITERS, NCOL), v(ITERS, GR), v(ITERS, NROW), v(ITERS), v(ITERS, 2, NCOL), v(ITERS, 2),
            v(GR, 2), v(2), pltpu.VMEM((GR, BLK, 128), F32), v(5),
            dma, dma((NCOL,)), dma((NCOL,)), dma((ITERS, NCOL)), dma((ITERS, NROW)), dma((ITERS, 3)),
            dma((ITERS, GR)), dma((ITERS,)), dma((ITERS, NCOL)), dma((ITERS, NROW)),
            dma((ITERS, 2, NCOL)), dma((ITERS, 2, NCOL)), dma((NCOL,)), dma((GR,)),
        ],
        compiler_params=pltpu.CompilerParams(collective_id=1, has_side_effects=True, vmem_limit_bytes=40 * 2**20),
        name="gradients",
    )(tile, dchunk, xinv, pmat, rhs)


def body(jac_row, jac_col, point_inv, pair_counts, camera_blocks, right_side):
    tile, dchunk, pg = form(minv_table(point_inv, pair_counts), stack_rows(jac_row), stack_rows(jac_col),
                            camera_blocks.reshape(NCOL, CH, BLK))
    xinv, pmat = inverse(pg.reshape(BLK, BLK), tile)
    wide = 128 * LT
    rhs = jnp.pad(right_side, ((0, 0), (0, wide - BLK))).reshape(GR, LT, 128)
    rhs = jnp.pad(rhs, ((0, 0), (0, 8 - LT), (0, 0)))
    diag, sol, res = gradients(tile, dchunk, xinv, pmat, rhs)
    back = lambda v: v[:, :LT].reshape(GR, wide)[:, :BLK]
    return tile[:, None], diag.reshape(GR, BLK, BLK), back(sol), back(res)


def solution(mesh):
    return jax.shard_map(
        body,
        mesh=mesh,
        in_specs=(
            P("row", "col", None, None, None, None, None),
            P("row", "col", None, None, None, None, None),
            P("row", "col", None, None, None, None),
            P("row", "col", None, None),
            P("row", None, None),
            P("row", None),
        ),
        out_specs=(
            P("row", "col", None, None),
            P("row", None, None),
            P("row", None),
            P("row", None),
        ),
        check_vma=False,
    )
```

```python
import jax
import jax.numpy as jnp
from jax import lax
from jax.experimental import pallas as pl
from jax.experimental.pallas import tpu as pltpu
from jax.sharding import PartitionSpec as P

MESH = pl.DeviceIdType.MESH
F32 = jnp.float32
BF16 = jnp.bfloat16
NROW, NCOL, GR, SLOT, BLK = 8, 16, 2, 64, 576
SIDE = 4
K3 = 3 * SLOT
CH = 72
WIDE = 640
CUT = 256
REST = BLK - CUT
ITERS = 2

OFF = (2, 1, 3, 0)
ORDER = [(u, v) for t in range(SIDE) for u in range(SIDE) for v in range(SIDE) if min(u, v) == t]


def pick(table, n):
    return sum(jnp.where(n == i, value, 0) for i, value in enumerate(table))


def tn(lhs, rhs):
    return lax.dot_general(lhs, rhs, (((0,), (0,)), ((), ())), preferred_element_type=F32)


def each(lo, hi, fn):
    def body(i, n):
        fn(i)
        return n
    lax.fori_loop(lo, hi, body, 0)


def remote(src, dst, ss, rs, dev):
    return pltpu.make_async_remote_copy(src_ref=src, dst_ref=dst, send_sem=ss, recv_sem=rs, device_id=dev,
                                        device_id_type=MESH)


def form_kernel(minv, wrow, wcol, cam, tile, dchunk, terms, pg_out,
                lrow, lcol, limg, rrow, rimg, big, ta_s, tb_s, ta_r, tb_r, p_s, p_r, h0_r, h1_r, srow, qrow, pg, camv, tsum,
                l_sem, cam_sem, w_send, w_recv, i_send, i_recv, t_send, t_recv, p_send, p_recv, h_send, h_recv,
                rs_send, rs_recv, pg_send, pg_recv):
    r = lax.axis_index("row")
    c = lax.axis_index("col")
    z, x = c // SIDE, lax.rem(c, SIDE)
    cg = c // GR
    g = GR * r + c // NROW
    part = c % NROW

    barrier = pltpu.get_barrier_semaphore()

    def greet(i):
        pl.semaphore_signal(barrier, inc=1, device_id=(r, lax.rem(c + i, NCOL)), device_id_type=MESH)

        @pl.when(i < NROW)
        def _():
            pl.semaphore_signal(barrier, inc=1, device_id=(lax.rem(r + i, NROW), c), device_id_type=MESH)
    each(1, NCOL, greet)

    def at(dz, dx):
        return lax.rem(z + dz, SIDE) * SIDE + lax.rem(x + dx, SIDE)

    def place(n):
        u1, v1 = pick([o[0] for o in ORDER], n), pick([o[1] for o in ORDER], n)
        return u1, v1, pick([OFF[o[0]] for o in ORDER], n), pick([OFF[o[1]] for o in ORDER], n)

    def loads(n):
        _, _, u, v = place(n)
        slot = lax.rem(n, 2)
        return [pltpu.make_async_copy(src.at[at(u, v)], dst.at[slot], l_sem.at[k, slot])
                for k, (src, dst) in enumerate(((wrow, lrow), (wcol, lcol)))]

    def sends(n, a):
        u1, v1, u, v = place(n)
        d, t = (u, v1) if a == 0 else (v, u1)
        dev = (r, at(u, 0) if a == 0 else at(0, v))
        k = jnp.maximum(d - 1, 0)
        rows = pl.ds(K3 * k, K3)
        return d > 0, [
            remote(wrow.at[at(u, v), pl.ds(K3 * a, K3)], rrow.at[a, t, rows], w_send.at[a, n], w_recv.at[a, t, k], dev),
            remote(limg.at[n, a], rimg.at[a, t, rows], i_send.at[a, n], i_recv.at[a, t, k], dev)]

    def term(n):
        _, _, u, v = place(n)
        j = at(u, v)
        dev = (j // GR, c)
        s = lax.rem(j, GR)
        return j, [remote(ta_s.at[n], ta_r.at[r, s], t_send.at[0, n], t_recv.at[0, r, s], dev),
                   remote(tb_s.at[n], tb_r.at[r, s], t_send.at[1, n], t_recv.at[1, r, s], dev)]

    cam_copy = pltpu.make_async_copy(cam.at[c], camv, cam_sem)
    cam_copy.start()
    for cp in loads(0):
        cp.start()
    tile[...] = jnp.zeros_like(tile)
    row_i = lax.broadcasted_iota(jnp.int32, (SLOT, K3), 0)
    col_i = lax.broadcasted_iota(jnp.int32, (SLOT, K3), 1)
    eye = jnp.where(lax.rem(col_i, SLOT) == row_i, 1.0, 0.0).astype(F32)
    pl.semaphore_wait(barrier, NCOL - 1 + NROW - 1)

    def local(n):
        _, _, u, v = place(n)
        slot = lax.rem(n, 2)

        @pl.when(n + 1 < NCOL)
        def _():
            for cp in loads(n + 1):
                cp.start()
        for a in range(GR):
            goes, cps = sends(n, a)

            @pl.when(goes)
            def _():
                cps[0].start()
        for cp in loads(n):
            cp.wait()
        j = at(u, v)
        top, bot = [], []
        for a in range(GR):
            ent = minv[j, 8 * a:8 * a + 8, :].astype(F32)
            for k in range(3):
                big[a, SLOT * k:SLOT * (k + 1), :] = (eye * ent[k:k + 1, :]).astype(BF16)
            wr = lrow[slot, K3 * a:K3 * (a + 1), :]
            wc = lcol[slot, K3 * a:K3 * (a + 1), :]
            limg[n, a] = jnp.dot(big[a], wc, preferred_element_type=F32).astype(BF16)
            goes, cps = sends(n, a)

            @pl.when(goes)
            def _():
                cps[1].start()
            ri = jnp.dot(big[a], wr, preferred_element_type=F32).astype(BF16)
            tile[a, CUT:, :] += tn(wr[:, CUT:], ri)
            tile[a, :CUT, :CUT] += tn(wr[:, :CUT], ri[:, :CUT])
        wc0, wc1 = lcol[slot, :K3, :], lcol[slot, K3:, :]
        ta_s[n] = (tn(wc0[:, CUT:], limg[n, 0]) + tn(wc1[:, CUT:], limg[n, 1])).astype(BF16)
        tb_s[n] = (tn(wc0[:, :CUT], limg[n, 0, :, :CUT]) + tn(wc1[:, :CUT], limg[n, 1, :, :CUT])).astype(BF16)
        _, cps = term(n)

        @pl.when(j // GR != r)
        def _():
            for cp in cps:
                cp.start()

        @pl.when(j // GR == r)
        def _():
            s = lax.rem(j, GR)
            ta_r[r, s] = ta_s[n]
            tb_r[r, s] = tb_s[n]
    each(0, NCOL, local)

    def along(a, off):
        return (r, at(0, off) if a == 0 else at(off, 0))

    def own_rows(a, t):
        j = at(0, OFF[t]) if a == 0 else at(OFF[t], 0)
        return pltpu.make_async_copy(wrow.at[j, pl.ds(K3 * a, K3)], lrow.at[a, pl.ds(0, K3)], l_sem.at[0, a])

    def arrive(a, t):
        for k in range(SIDE - 1):
            rows = pl.ds(K3 * k, K3)
            dev = (r, at(k + 1, 0))
            remote(wrow.at[0, pl.ds(0, K3)], rrow.at[a, t, rows], w_send.at[a, 0], w_recv.at[a, t, k], dev).wait_recv()
            remote(limg.at[0, a], rimg.at[a, t, rows], i_send.at[a, 0], i_recv.at[a, t, k], dev).wait_recv()

    def partial(a, t, lo, hi):
        own = ORDER.index((SIDE - 1, t) if a == 0 else (t, SIDE - 1))
        return tn(rrow[a, t, :, lo:hi], rimg[a, t]) + tn(lrow[a, :K3, lo:hi], limg[own, a])

    blocks = ((0, 256), (256, 512), (512, 576))

    def relays(a):
        return [remote(p_s.at[a, 0, pl.ds(0, CUT)], h0_r.at[a], h_send.at[a, 0], h_recv.at[a, 0], along(a, 1)),
                remote(p_s.at[a, 0, pl.ds(CUT, REST)], h1_r.at[a], h_send.at[a, 1], h_recv.at[a, 1], along(a, 3))]

    def p_copy(a, t):
        return remote(p_s.at[a, t], p_r.at[a, t - 1], p_send.at[a, t - 1], p_recv.at[a, t - 1], along(a, OFF[t]))

    def pairs(t):
        for a in range(GR):
            own_rows(a, t).start()
        for a in range(GR):
            own_rows(a, t).wait()
            arrive(a, t)
            if t > 0:
                relays(a)[t - 1].wait_recv()
            for lo, hi in blocks:
                out = partial(a, t, lo, hi)
                if t == 1 and hi <= CUT:
                    out = out + h0_r[a, lo:hi, :].astype(F32)
                if t == 2 and lo >= CUT:
                    out = out + h1_r[a, lo - CUT:hi - CUT, :].astype(F32)
                p_s[a, t, lo:hi, :] = out.astype(BF16)
            for cp in relays(a) if t == 0 else [p_copy(a, t)]:
                cp.start()
    for t in range(SIDE - 1):
        pairs(t)

    def term_sum(i):
        for s in range(GR):
            @pl.when(i != r)
            def _():
                remote(ta_s.at[0], ta_r.at[i, s], t_send.at[0, 0], t_recv.at[0, i, s], (i, c)).wait_recv()
                remote(tb_s.at[0], tb_r.at[i, s], t_send.at[1, 0], t_recv.at[1, i, s], (i, c)).wait_recv()
            tile[s, CUT:, :] += ta_r[i, s].astype(F32)
            tile[s, :CUT, :CUT] += tb_r[i, s].astype(F32)
    each(0, NROW, term_sum)
    for a in range(GR):
        tile[a, :CUT, CUT:] = tile[a, CUT:, :CUT].T
    for m in range(NCOL):
        a, i = divmod(m, NROW)
        srow[m] = tile[a, CH * i:CH * (i + 1), :].astype(BF16)

    def row_copy(d):
        j = lax.rem(c + d, NCOL)
        return remote(srow.at[j], qrow.at[d], rs_send.at[d], rs_recv.at[d], (r, j))
    each(1, NCOL, lambda d: row_copy(d).start())

    last = SIDE - 1
    for a in range(GR):
        own_rows(a, last).start()
    for a in range(GR):
        own_rows(a, last).wait()
        arrive(a, last)
        for lo, hi in blocks:
            tile[a, lo:hi, :] = partial(a, last, lo, hi)

    tsum[...] = srow[c].astype(F32)

    def row_sum(d):
        row_copy(d).wait_recv()
        tsum[...] += qrow[d].astype(F32)
    each(1, NCOL, row_sum)
    cam_copy.wait()
    total = tsum[...]
    short = total.astype(BF16)
    on = (lax.broadcasted_iota(jnp.int32, (CH, BLK), 0) + part * CH) == lax.broadcasted_iota(jnp.int32, (CH, BLK), 1)
    rest = jnp.sum(jnp.where(on, total - short.astype(F32), 0.0), axis=1, keepdims=True).astype(BF16).astype(F32)
    terms[:, :BLK] = short
    terms[:, BLK:] = jnp.broadcast_to(rest, (CH, WIDE - BLK)).astype(BF16)
    dchunk[...] = camv[...] - (short.astype(F32) + jnp.where(on, rest, 0.0))

    is_p = cg == r

    def pg_copy(i):
        return remote(dchunk, pg.at[i], pg_send, pg_recv.at[i], (r, g))

    @pl.when(g != c)
    def _():
        pg_copy(part).start()

    for t in (1, 2):
        for a in range(GR):
            p_copy(a, t).wait_recv()
            tile[a] += p_r[a, t - 1].astype(F32)

    def gather(i):
        src_c = (c % GR) * NROW + i

        @pl.when(jnp.logical_and(is_p, src_c != c))
        def _():
            pg_copy(i).wait_recv()
            pg_out[i] = pg[i]

        @pl.when(jnp.logical_and(is_p, src_c == c))
        def _():
            pg_out[i] = dchunk[...]

        @pl.when(jnp.logical_not(is_p))
        def _():
            rows = lax.broadcasted_iota(jnp.int32, (CH, BLK), 0) + i * CH
            cols = lax.broadcasted_iota(jnp.int32, (CH, BLK), 1)
            pg_out[i] = jnp.where(rows == cols, 1.0, 0.0).astype(F32)
    each(0, NROW, gather)

    @pl.when(g != c)
    def _():
        pg_copy(part).wait_send()

    def drain(n):
        for a in range(GR):
            goes, cps = sends(n, a)

            @pl.when(goes)
            def _():
                for cp in cps:
                    cp.wait_send()
        j, cps = term(n)

        @pl.when(j // GR != r)
        def _():
            for cp in cps:
                cp.wait_send()

        @pl.when(n > 0)
        def _():
            row_copy(n).wait_send()
    each(0, NCOL, drain)
    for a in range(GR):
        for cp in relays(a) + [p_copy(a, 1), p_copy(a, 2)]:
            cp.wait_send()


def form(minv, wrow, wcol, cam):
    any_ = pl.BlockSpec(memory_space=pl.ANY)
    vm = pl.BlockSpec(memory_space=pltpu.VMEM)
    dma = pltpu.SemaphoreType.DMA
    legs = SIDE - 1
    return pl.pallas_call(
        form_kernel,
        out_shape=(jax.ShapeDtypeStruct((GR, BLK, BLK), F32), jax.ShapeDtypeStruct((CH, BLK), F32),
                   jax.ShapeDtypeStruct((CH, WIDE), BF16), jax.ShapeDtypeStruct((NROW, CH, BLK), F32)),
        in_specs=[vm] + [any_] * 3,
        out_specs=(vm, vm, vm, vm),
        scratch_shapes=[
            pltpu.VMEM((2, GR * K3, BLK), BF16),
            pltpu.VMEM((2, GR * K3, BLK), BF16),
            pltpu.VMEM((NCOL, GR, K3, BLK), BF16),
            pltpu.VMEM((GR, SIDE, legs * K3, BLK), BF16),
            pltpu.VMEM((GR, SIDE, legs * K3, BLK), BF16),
            pltpu.VMEM((GR, K3, K3), BF16),
            pltpu.VMEM((NCOL, REST, BLK), BF16),
            pltpu.VMEM((NCOL, CUT, CUT), BF16),
            pltpu.VMEM((NROW, GR, REST, BLK), BF16),
            pltpu.VMEM((NROW, GR, CUT, CUT), BF16),
            pltpu.VMEM((GR, legs, BLK, BLK), BF16),
            pltpu.VMEM((GR, 2, BLK, BLK), BF16),
            pltpu.VMEM((GR, CUT, BLK), BF16),
            pltpu.VMEM((GR, REST, BLK), BF16),
            pltpu.VMEM((NCOL, CH, BLK), BF16),
            pltpu.VMEM((NCOL, CH, BLK), BF16),
            pltpu.VMEM((NROW, CH, BLK), F32),
            pltpu.VMEM((CH, BLK), F32),
            pltpu.VMEM((CH, BLK), F32),
            dma((2, 2)), dma, dma((GR, NCOL)), dma((GR, SIDE, legs)), dma((GR, NCOL)), dma((GR, SIDE, legs)),
            dma((2, NCOL)), dma((2, NROW, GR)), dma((GR, 2)), dma((GR, 2)), dma((GR, 2)), dma((GR, 2)),
            dma((NCOL,)), dma((NCOL,)), dma, dma((NROW,)),
        ],
        compiler_params=pltpu.CompilerParams(collective_id=0, has_side_effects=True, vmem_limit_bytes=62 * 2**20),
        name="form",
    )(minv, wrow, wcol, cam)


def minv_table(point_inv, pair_counts):
    inv = point_inv.reshape(NCOL, GR, SLOT, 3, 3)
    live = lax.broadcasted_iota(jnp.int32, (NCOL, GR, SLOT), 2) < pair_counts.reshape(NCOL, GR)[:, :, None]
    masked = inv * live[..., None, None].astype(BF16)
    rows = jnp.transpose(masked, (0, 1, 3, 4, 2)).reshape(NCOL, GR, 3, K3)
    return jnp.pad(rows, ((0, 0), (0, 0), (0, 5), (0, 0))).reshape(NCOL, 16, K3)


def stack_rows(jac):
    return jnp.transpose(jac.reshape(jac.shape[2:]), (0, 1, 3, 2, 4)).reshape(NCOL, GR * K3, BLK)


def mm(lhs, rhs):
    return jnp.dot(lhs.astype(BF16), rhs.astype(BF16), preferred_element_type=F32)


def mm_high(lhs, rhs):
    return jnp.dot(lhs, rhs, preferred_element_type=F32, precision=lax.Precision.HIGHEST)


def inverse_kernel(pg, tile, xinv, pmat, tile_out, both, e, y, res, sem, out_sem):
    r = lax.axis_index("row")
    c = lax.axis_index("col")
    is_p = (c // GR == r).astype(F32)
    cp = pltpu.make_async_copy(tile, both, sem)
    keep = pltpu.make_async_copy(both, tile_out, out_sem)
    cp.start()
    rows = lax.broadcasted_iota(jnp.int32, (BLK, BLK), 0)
    cols = lax.broadcasted_iota(jnp.int32, (BLK, BLK), 1)
    eye = jnp.where(rows == cols, 1.0, 0.0).astype(F32)
    cp.wait()
    keep.start()
    wide = 0.5 * pg[...] - both[c % GR] * is_p
    p = wide + wide.T
    pmat[...] = p
    dd = p * eye
    s_row = lax.rsqrt(jnp.sum(dd, axis=0, keepdims=True))
    s_col = lax.rsqrt(jnp.sum(dd, axis=1, keepdims=True))
    b = p * s_row * s_col
    e[...] = eye - b
    e2 = mm(e[...], e[...])
    f2 = jnp.sum(e2 * e2)

    @pl.when(f2 < 0.9)
    def _():
        y[...] = e[...] + e2 + mm(e[...], e2)

    @pl.when(jnp.logical_not(f2 < 0.9))
    def _():
        big = jnp.max(jnp.sum(jnp.abs(eye - e[...]), axis=1, keepdims=True))
        y[...] = eye * (1.0 / big - 1.0)

    def residual(mul):
        out = e[...] - y[...] + mul(y[...], e[...])
        res[...] = out
        return jnp.sum(out * out)

    def more(state):
        step, size = state
        return jnp.logical_and(size > 1.6e-5, step < 64)

    def newton(state):
        step, _ = state

        def low():
            y[...] = y[...] + res[...] + mm(res[...], y[...])
            return residual(mm)

        def high():
            y[...] = y[...] + res[...] + mm_high(res[...], y[...])
            return residual(mm_high)
        return step + 1, lax.cond(step < 6, low, high)
    lax.while_loop(more, newton, (jnp.int32(0), residual(mm)))
    xinv[...] = (eye + y[...]) * s_row * s_col
    keep.wait()


def inverse(pg, tile):
    vm = pl.BlockSpec(memory_space=pltpu.VMEM)
    sq = jax.ShapeDtypeStruct((BLK, BLK), F32)
    return pl.pallas_call(
        inverse_kernel,
        out_shape=(sq, sq, jax.ShapeDtypeStruct((GR, BLK, BLK), F32)),
        in_specs=[vm, pl.BlockSpec(memory_space=pl.ANY)],
        out_specs=(vm, vm, pl.BlockSpec(memory_space=pl.ANY)),
        scratch_shapes=[pltpu.VMEM((GR, BLK, BLK), F32)] + [pltpu.VMEM((BLK, BLK), F32)] * 3 + [pltpu.SemaphoreType.DMA] * 2,
        compiler_params=pltpu.CompilerParams(vmem_limit_bytes=48 * 2**20),
        name="inverse",
    )(pg, tile)


LT = 5
REFINE = 2


def lanes(t):
    return 128 * t, min(128 * (t + 1), BLK)


def spread(mat, vec):
    rows = mat.shape[0]
    acc = jnp.zeros((rows, 128), F32)
    for t in range(LT):
        lo, hi = lanes(t)
        part = mat[:, lo:hi] * vec[t:t + 1, :hi - lo]
        if hi - lo < 128:
            part = jnp.concatenate([part, jnp.zeros((rows, 128 - (hi - lo)), F32)], axis=1)
        acc = acc + part
    return acc


def fold(acc):
    out = []
    for t in range(LT):
        lo, hi = lanes(t)
        blk = acc[lo:hi, :]
        if hi - lo < 128:
            blk = jnp.concatenate([blk, jnp.zeros((128 - (hi - lo), 128), F32)], axis=0)
        out.append(jnp.sum(blk.T, axis=0, keepdims=True))
    return jnp.concatenate(out + [jnp.zeros((8 - LT, 128), F32)], axis=0)


def columns(vec):
    return jnp.concatenate([jnp.broadcast_to(vec[t:t + 1, :], (128, 128)).T for t in range(LT)], axis=0)


def matvec(mat, vec):
    return fold(spread(mat, vec))


def cg_kernel(tile, dchunk, xinv, pmat, rhs, sol, resid,
              zbuf, zsrc, cbuf, csrc, bbuf, bsrc, sbuf, ssrc, fbuf, fsrc, acc, state,
              zr_send, zc_send, z_recv, c_send, b_send, c_recv, b_recv,
              s_send, s_recv, f_send, f_recv):
    r = lax.axis_index("row")
    c = lax.axis_index("col")
    ap = c % GR
    cg = c // GR
    half = c // NROW
    part = c % NROW
    is_p = cg == r
    not_p = jnp.logical_not(is_p)

    barrier = pltpu.get_barrier_semaphore()

    def greet(i, n):
        pl.semaphore_signal(barrier, inc=1, device_id=(r, lax.rem(c + i, NCOL)), device_id_type=MESH)

        @pl.when(i < NROW)
        def _():
            pl.semaphore_signal(barrier, inc=1, device_id=(lax.rem(r + i, NROW), c), device_id_type=MESH)

        @pl.when(is_p)
        def _():
            other = lax.rem(c + i, NCOL)
            pl.semaphore_signal(barrier, inc=1, device_id=(other // GR, other), device_id_type=MESH)
        return n
    lax.fori_loop(1, NCOL, greet, 0)
    pl.semaphore_wait(barrier, NCOL - 1 + NROW - 1 + (NCOL - 1) * is_p.astype(jnp.int32))

    def zr_copy(it, d):
        return remote(zsrc.at[it], zbuf.at[it, ap], zr_send.at[it, d], z_recv.at[it, ap], (r, lax.rem(c + d, NCOL)))

    def zc_copy(it, d):
        return remote(zsrc.at[it], zbuf.at[it, 2], zc_send.at[it, d], z_recv.at[it, 2], (lax.rem(r + d, NROW), c))

    def z_from(it, slot):
        return remote(zsrc.at[it], zbuf.at[it, slot], zr_send.at[it, 0], z_recv.at[it, slot], (lax.rem(r + 1, NROW), c))

    def s_copy(k, d):
        other = lax.rem(c + d, NCOL)
        return remote(ssrc.at[k], sbuf.at[k, c], s_send.at[k, d], s_recv.at[k], (other // GR, other))

    def c_copy(it, a):
        return remote(csrc.at[it, a], cbuf.at[it, c], c_send.at[it, a], c_recv.at[it], (r, GR * r + a))

    def b_copy(it):
        return remote(bsrc.at[it], bbuf.at[it, r], b_send.at[it], b_recv.at[it], (cg, c))

    def take(buf, sem, count):
        pltpu.make_async_copy(buf.at[pl.ds(0, count)], buf.at[pl.ds(0, count)], sem).wait()

    def f_copy(d):
        return remote(fsrc, fbuf.at[ap], f_send.at[d], f_recv.at[ap], (r, lax.rem(c + d, NCOL)))

    def f_from(a):
        return remote(fsrc, fbuf.at[a], f_send.at[0], f_recv.at[a], (r, GR * r + a))

    def exchange(k, top, bottom):
        upper = lax.broadcasted_iota(jnp.int32, (8, 128), 0) < 4
        ssrc[k] = jnp.where(upper, jnp.sum(top), jnp.sum(bottom))
        each(1, NCOL, lambda d: s_copy(k, d).start())

    def totals(k):
        take(sbuf.at[k], s_recv.at[k], NCOL - 1)
        sbuf[k, c] = ssrc[k]
        both = jnp.sum(sbuf[k], axis=0)
        return both[0:1, :], both[4:5, :]

    def apply(vec):
        out = matvec(xinv, vec)
        for _ in range(REFINE):
            out = out + matvec(xinv, vec - matvec(pmat, out))
        return out

    def spread_out(it, vec):
        zsrc[it] = vec
        each(1, NCOL, lambda d: zr_copy(it, d).start())
        each(1, NROW, lambda d: zc_copy(it, d).start())
        zbuf[it, ap] = vec
        zbuf[it, 2] = vec

    def products(it):
        for slot in range(3):
            @pl.when(not_p if slot == 2 else c != GR * r + slot)
            def _():
                z_from(it, slot).wait_recv()

        zc = zbuf[it, 2]
        back = [jnp.zeros((1, hi - lo), F32) for lo, hi in map(lanes, range(LT))]
        for a in range(GR):
            acc[a] = -spread(tile[a], zc)
            zcol = columns(zbuf[it, a])
            for t in range(LT):
                lo, hi = lanes(t)
                back[t] = back[t] + jnp.sum(tile[a, :, lo:hi] * zcol[:BLK, :hi - lo], axis=0, keepdims=True)
        rows = pl.ds(pl.multiple_of(part * CH, 8), CH)
        acc[half, rows, :] += spread(dchunk[...], zbuf[it, half])
        back[LT - 1] = jnp.concatenate([back[LT - 1], jnp.zeros((1, 128 * LT - BLK), F32)], axis=1)
        bsrc[it] = jnp.concatenate(back + [jnp.zeros((8 - LT, 128), F32)], axis=0)

        @pl.when(not_p)
        def _():
            b_copy(it).start()
        for a in range(GR):
            csrc[it, a] = fold(acc[a])

            @pl.when(c != GR * r + a)
            def _():
                c_copy(it, a).start()

    def collect(it):
        take(cbuf.at[it], c_recv.at[it], NCOL - 1)
        take(bbuf.at[it], b_recv.at[it], NROW - 1)
        cbuf[it, c] = csrc[it, ap]
        bbuf[it, r] = bsrc[it]
        return jnp.sum(cbuf[it], axis=0) - jnp.sum(bbuf[it], axis=0)

    @pl.when(is_p)
    def _():
        spread_out(0, apply(rhs[ap]))
    products(0)

    @pl.when(is_p)
    def _():
        image = collect(0)
        state[0] = image
        spread_out(1, apply(image))
        exchange(0, rhs[ap] * zsrc[0], zsrc[0] * image)
    products(1)

    @pl.when(is_p)
    def _():
        first, image = zsrc[0], state[0]
        rz, curve = totals(0)
        alpha = rz / curve
        res = rhs[ap] - alpha * image
        second = first - alpha * zsrc[1]
        exchange(1, res * second, res * second)
        moved = image - alpha * collect(1)
        rz_next, _ = totals(1)
        beta = rz_next / rz
        direction = second + beta * first
        image = moved + beta * image
        exchange(2, direction * image, direction * image)
        curve, _ = totals(2)
        step = rz_next / curve
        fsrc[0] = alpha * first + step * direction
        fsrc[1] = res - step * image
        each(1, NCOL, lambda d: f_copy(d).start())
        fbuf[ap] = fsrc[...]

    for a in range(GR):
        @pl.when(c != GR * r + a)
        def _():
            f_from(a).wait_recv()
        sol[a] = fbuf[a, 0]
        resid[a] = fbuf[a, 1]

    for it in range(ITERS):
        @pl.when(not_p)
        def _():
            b_copy(it).wait_send()
        for a in range(GR):
            @pl.when(c != GR * r + a)
            def _():
                c_copy(it, a).wait_send()

    @pl.when(is_p)
    def _():
        for it in range(ITERS):
            each(1, NCOL, lambda d: zr_copy(it, d).wait_send())
            each(1, NROW, lambda d: zc_copy(it, d).wait_send())
        for k in range(3):
            each(1, NCOL, lambda d: s_copy(k, d).wait_send())
        each(1, NCOL, lambda d: f_copy(d).wait_send())


def gradients(tile, dchunk, xinv, pmat, rhs):
    vm = pl.BlockSpec(memory_space=pltpu.VMEM)
    dma = pltpu.SemaphoreType.DMA
    v = lambda *lead: pltpu.VMEM((*lead, 8, 128), F32)
    vec = jax.ShapeDtypeStruct((GR, 8, 128), F32)
    return pl.pallas_call(
        cg_kernel,
        out_shape=(vec, vec),
        in_specs=[vm] * 5,
        out_specs=(vm, vm),
        scratch_shapes=[
            v(ITERS, 3), v(ITERS), v(ITERS, NCOL), v(ITERS, GR), v(ITERS, NROW), v(ITERS), v(3, NCOL), v(3),
            v(GR, 2), v(2), pltpu.VMEM((GR, BLK, 128), F32), v(1),
            dma((ITERS, NCOL)), dma((ITERS, NROW)), dma((ITERS, 3)),
            dma((ITERS, GR)), dma((ITERS,)), dma((ITERS,)), dma((ITERS,)),
            dma((3, NCOL)), dma((3,)), dma((NCOL,)), dma((GR,)),
        ],
        compiler_params=pltpu.CompilerParams(collective_id=1, has_side_effects=True, vmem_limit_bytes=40 * 2**20),
        name="gradients",
    )(tile, dchunk, xinv, pmat, rhs)


def subtract_kernel(cam, terms, out):
    rows = lax.broadcasted_iota(jnp.int32, (CH, BLK), 0)
    cols = lax.broadcasted_iota(jnp.int32, (CH, BLK), 1)
    for a in range(GR):
        for lo in range(0, BLK, CH):
            part = terms[a, lo:lo + CH, :]
            rest = part[:, BLK:BLK + 1].astype(F32)
            out[a, lo:lo + CH, :] = cam[a, lo:lo + CH, :] - (
                part[:, :BLK].astype(F32) + jnp.where(rows + lo == cols, rest, 0.0))


def subtract(cam, terms):
    vm = pl.BlockSpec(memory_space=pltpu.VMEM)
    return pl.pallas_call(
        subtract_kernel,
        out_shape=jax.ShapeDtypeStruct((GR, BLK, BLK), F32),
        in_specs=[vm, vm],
        out_specs=vm,
        compiler_params=pltpu.CompilerParams(vmem_limit_bytes=24 * 2**20),
        name="subtract",
    )(cam, terms)


def body(jac_row, jac_col, point_inv, pair_counts, camera_blocks, right_side):
    tile, dchunk, terms, pg = form(minv_table(point_inv, pair_counts), stack_rows(jac_row), stack_rows(jac_col),
                                   camera_blocks.reshape(NCOL, CH, BLK))
    xinv, pmat, pairs = inverse(pg.reshape(BLK, BLK), tile)
    wide = 128 * LT
    rhs = jnp.pad(right_side, ((0, 0), (0, wide - BLK))).reshape(GR, LT, 128)
    rhs = jnp.pad(rhs, ((0, 0), (0, 8 - LT), (0, 0)))
    diag = subtract(camera_blocks, lax.all_gather(terms, "col", axis=0, tiled=True).reshape(GR, BLK, WIDE))
    sol, res = gradients(tile, dchunk, xinv, pmat, rhs)
    back = lambda v: v[:, :LT].reshape(GR, wide)[:, :BLK]
    return pairs[:, None], diag, back(sol), back(res)


def solution(mesh):
    return jax.shard_map(
        body,
        mesh=mesh,
        in_specs=(
            P("row", "col", None, None, None, None, None),
            P("row", "col", None, None, None, None, None),
            P("row", "col", None, None, None, None),
            P("row", "col", None, None),
            P("row", None, None),
            P("row", None),
        ),
        out_specs=(
            P("row", "col", None, None),
            P("row", None, None),
            P("row", None),
            P("row", None),
        ),
        check_vma=False,
    )
```

```python
import jax
import jax.numpy as jnp
from jax import lax
from jax.experimental import pallas as pl
from jax.experimental.pallas import tpu as pltpu
from jax.sharding import PartitionSpec as P

MESH = pl.DeviceIdType.MESH
F32 = jnp.float32
BF16 = jnp.bfloat16
NROW, NCOL, GR, SLOT, BLK = 8, 16, 2, 64, 576
SIDE = 4
K3 = 3 * SLOT
CH = 72
WIDE = 640
MAIN = 512
CUT = 256
REST = BLK - CUT
ITERS = 2

OFF = (2, 1, 3, 0)
ORDER = [(u, v) for t in range(SIDE) for u in range(SIDE) for v in range(SIDE) if min(u, v) == t]


def pick(table, n):
    return sum(jnp.where(n == i, value, 0) for i, value in enumerate(table))


def tn(lhs, rhs):
    return lax.dot_general(lhs, rhs, (((0,), (0,)), ((), ())), preferred_element_type=F32)


def each(lo, hi, fn):
    def body(i, n):
        fn(i)
        return n
    lax.fori_loop(lo, hi, body, 0)


def remote(src, dst, ss, rs, dev):
    return pltpu.make_async_remote_copy(src_ref=src, dst_ref=dst, send_sem=ss, recv_sem=rs, device_id=dev,
                                        device_id_type=MESH)


def form_kernel(minv, wrow, wcol, cam, tile, dchunk, terms, pg_out,
                lrow, lcol, limg, rrow, rimg, big, ta_s, tb_s, ta_r, tb_r, p_s, p_r, h0_r, h1_r, srow, qrow, pg, camv, tsum, dsend,
                l_sem, cam_sem, w_send, w_recv, i_send, i_recv, t_send, t_recv, p_send, p_recv, h_send, h_recv,
                rs_send, rs_recv, pg_send, pg_recv):
    r = lax.axis_index("row")
    c = lax.axis_index("col")
    z, x = c // SIDE, lax.rem(c, SIDE)
    cg = c // GR
    g = GR * r + c // NROW
    part = c % NROW

    barrier = pltpu.get_barrier_semaphore()

    def greet(i):
        pl.semaphore_signal(barrier, inc=1, device_id=(r, lax.rem(c + i, NCOL)), device_id_type=MESH)

        @pl.when(i < NROW)
        def _():
            pl.semaphore_signal(barrier, inc=1, device_id=(lax.rem(r + i, NROW), c), device_id_type=MESH)
    each(1, NCOL, greet)

    def at(dz, dx):
        return lax.rem(z + dz, SIDE) * SIDE + lax.rem(x + dx, SIDE)

    def place(n):
        u1, v1 = pick([o[0] for o in ORDER], n), pick([o[1] for o in ORDER], n)
        return u1, v1, pick([OFF[o[0]] for o in ORDER], n), pick([OFF[o[1]] for o in ORDER], n)

    def loads(n):
        _, _, u, v = place(n)
        slot = lax.rem(n, 2)
        return [pltpu.make_async_copy(src.at[at(u, v)], dst.at[slot], l_sem.at[k, slot])
                for k, (src, dst) in enumerate(((wrow, lrow), (wcol, lcol)))]

    def sends(n, a):
        u1, v1, u, v = place(n)
        d, t = (u, v1) if a == 0 else (v, u1)
        dev = (r, at(u, 0) if a == 0 else at(0, v))
        k = jnp.maximum(d - 1, 0)
        rows = pl.ds(K3 * k, K3)
        return d > 0, [
            remote(wrow.at[at(u, v), pl.ds(K3 * a, K3), pl.ds(0, MAIN)], rrow.at[a, t, rows], w_send.at[a, n], w_recv.at[a, t, k], dev),
            remote(limg.at[n, a], rimg.at[a, t, rows], i_send.at[a, n], i_recv.at[a, t, k], dev)]

    def term(n):
        _, _, u, v = place(n)
        j = at(u, v)
        dev = (j // GR, c)
        s = lax.rem(j, GR)
        return j, [remote(ta_s.at[n], ta_r.at[r, s], t_send.at[0, n], t_recv.at[0, r, s], dev),
                   remote(tb_s.at[n], tb_r.at[r, s], t_send.at[1, n], t_recv.at[1, r, s], dev)]

    cam_copy = pltpu.make_async_copy(cam.at[c], camv, cam_sem)
    cam_copy.start()
    for cp in loads(0):
        cp.start()
    tile[...] = jnp.zeros_like(tile)
    for ref in (ta_s, srow):
        ref[:, :, MAIN:] = jnp.zeros((*ref.shape[:2], WIDE - MAIN), BF16)
    for a in range(GR):
        p_s[a, :, :, MAIN:] = jnp.zeros((SIDE - 1, BLK, WIDE - MAIN), BF16)
    dsend[:, MAIN:] = jnp.zeros((CH, WIDE - MAIN), F32)
    row_i = lax.broadcasted_iota(jnp.int32, (SLOT, K3), 0)
    col_i = lax.broadcasted_iota(jnp.int32, (SLOT, K3), 1)
    eye = jnp.where(lax.rem(col_i, SLOT) == row_i, 1.0, 0.0).astype(F32)
    pl.semaphore_wait(barrier, NCOL - 1 + NROW - 1)

    def local(n):
        _, _, u, v = place(n)
        slot = lax.rem(n, 2)

        @pl.when(n + 1 < NCOL)
        def _():
            for cp in loads(n + 1):
                cp.start()
        for a in range(GR):
            goes, cps = sends(n, a)

            @pl.when(goes)
            def _():
                cps[0].start()
        for cp in loads(n):
            cp.wait()
        j = at(u, v)
        top, bot = [], []
        for a in range(GR):
            ent = minv[j, 8 * a:8 * a + 8, :].astype(F32)
            for k in range(3):
                big[a, SLOT * k:SLOT * (k + 1), :] = (eye * ent[k:k + 1, :]).astype(BF16)
            wr = lrow[slot, K3 * a:K3 * (a + 1), :]
            wc = lcol[slot, K3 * a:K3 * (a + 1), :]
            ci = jnp.dot(big[a], wc, preferred_element_type=F32)
            limg[n, a, :, :MAIN] = ci[:, :MAIN].astype(BF16)
            limg[n, a, :, MAIN:] = jnp.concatenate([ci[:, MAIN:], wr[:, MAIN:].astype(F32)], axis=1).astype(BF16)
            goes, cps = sends(n, a)

            @pl.when(goes)
            def _():
                cps[1].start()
            ri = jnp.dot(big[a], wr, preferred_element_type=F32).astype(BF16)
            tile[a, CUT:, :] += tn(wr[:, CUT:], ri)
            tile[a, :CUT, :CUT] += tn(wr[:, :CUT], ri[:, :CUT])
        wc0, wc1 = lcol[slot, :K3, :], lcol[slot, K3:, :]
        ta_s[n, :, :BLK] = (tn(wc0[:, CUT:], limg[n, 0, :, :BLK]) + tn(wc1[:, CUT:], limg[n, 1, :, :BLK])).astype(BF16)
        tb_s[n] = (tn(wc0[:, :CUT], limg[n, 0, :, :CUT]) + tn(wc1[:, :CUT], limg[n, 1, :, :CUT])).astype(BF16)
        _, cps = term(n)

        @pl.when(j // GR != r)
        def _():
            for cp in cps:
                cp.start()

        @pl.when(j // GR == r)
        def _():
            s = lax.rem(j, GR)
            ta_r[r, s] = ta_s[n]
            tb_r[r, s] = tb_s[n]
    each(0, NCOL, local)

    def along(a, off):
        return (r, at(0, off) if a == 0 else at(off, 0))

    def own_rows(a, t):
        j = at(0, OFF[t]) if a == 0 else at(OFF[t], 0)
        return pltpu.make_async_copy(wrow.at[j, pl.ds(K3 * a, K3)], lrow.at[a, pl.ds(0, K3)], l_sem.at[0, a])

    def arrive(a, t):
        for k in range(SIDE - 1):
            rows = pl.ds(K3 * k, K3)
            dev = (r, at(k + 1, 0))
            remote(wrow.at[0, pl.ds(0, K3), pl.ds(0, MAIN)], rrow.at[a, t, rows], w_send.at[a, 0], w_recv.at[a, t, k], dev).wait_recv()
            remote(limg.at[0, a], rimg.at[a, t, rows], i_send.at[a, 0], i_recv.at[a, t, k], dev).wait_recv()

    def partial(a, t, lo, hi):
        own = ORDER.index((SIDE - 1, t) if a == 0 else (t, SIDE - 1))
        own = tn(lrow[a, :K3, lo:hi], limg[own, a, :, :BLK])
        if lo < MAIN:
            return own + tn(rrow[a, t, :, lo:hi], rimg[a, t, :, :BLK])
        return own + tn(rimg[a, t, :, lo:], rimg[a, t, :, :BLK])[hi - lo:, :]

    blocks = ((0, 256), (256, 512), (512, 576))

    def relays(a):
        return [remote(p_s.at[a, 0, pl.ds(0, CUT)], h0_r.at[a], h_send.at[a, 0], h_recv.at[a, 0], along(a, 1)),
                remote(p_s.at[a, 0, pl.ds(CUT, REST)], h1_r.at[a], h_send.at[a, 1], h_recv.at[a, 1], along(a, 3))]

    def p_copy(a, t):
        return remote(p_s.at[a, t], p_r.at[a, t - 1], p_send.at[a, t - 1], p_recv.at[a, t - 1], along(a, OFF[t]))

    def pairs(t):
        for a in range(GR):
            own_rows(a, t).start()
        for a in range(GR):
            own_rows(a, t).wait()
            arrive(a, t)
            if t > 0:
                relays(a)[t - 1].wait_recv()
            for lo, hi in blocks:
                out = partial(a, t, lo, hi)
                if t == 1 and hi <= CUT:
                    out = out + h0_r[a, lo:hi, :BLK].astype(F32)
                if t == 2 and lo >= CUT:
                    out = out + h1_r[a, lo - CUT:hi - CUT, :BLK].astype(F32)
                p_s[a, t, lo:hi, :BLK] = out.astype(BF16)
            for cp in relays(a) if t == 0 else [p_copy(a, t)]:
                cp.start()
    for t in range(SIDE - 1):
        pairs(t)

    def term_sum(i):
        for s in range(GR):
            @pl.when(i != r)
            def _():
                remote(ta_s.at[0], ta_r.at[i, s], t_send.at[0, 0], t_recv.at[0, i, s], (i, c)).wait_recv()
                remote(tb_s.at[0], tb_r.at[i, s], t_send.at[1, 0], t_recv.at[1, i, s], (i, c)).wait_recv()
            tile[s, CUT:, :] += ta_r[i, s, :, :BLK].astype(F32)
            tile[s, :CUT, :CUT] += tb_r[i, s].astype(F32)
    each(0, NROW, term_sum)
    for a in range(GR):
        tile[a, :CUT, CUT:] = tile[a, CUT:, :CUT].T
    for m in range(NCOL):
        a, i = divmod(m, NROW)
        srow[m, :, :BLK] = tile[a, CH * i:CH * (i + 1), :].astype(BF16)

    def row_copy(d):
        j = lax.rem(c + d, NCOL)
        return remote(srow.at[j], qrow.at[d], rs_send.at[d], rs_recv.at[d], (r, j))
    each(1, NCOL, lambda d: row_copy(d).start())

    last = SIDE - 1
    for a in range(GR):
        own_rows(a, last).start()
    for a in range(GR):
        own_rows(a, last).wait()
        arrive(a, last)
        for lo, hi in blocks:
            tile[a, lo:hi, :] = partial(a, last, lo, hi)

    tsum[...] = srow[c, :, :BLK].astype(F32)

    def row_sum(d):
        row_copy(d).wait_recv()
        tsum[...] += qrow[d, :, :BLK].astype(F32)
    each(1, NCOL, row_sum)
    cam_copy.wait()
    total = tsum[...]
    short = total.astype(BF16)
    on = (lax.broadcasted_iota(jnp.int32, (CH, BLK), 0) + part * CH) == lax.broadcasted_iota(jnp.int32, (CH, BLK), 1)
    rest = jnp.sum(jnp.where(on, total - short.astype(F32), 0.0), axis=1, keepdims=True).astype(BF16).astype(F32)
    terms[:, :BLK] = short
    terms[:, BLK:] = jnp.broadcast_to(rest, (CH, WIDE - BLK)).astype(BF16)
    dchunk[...] = camv[...] - (short.astype(F32) + jnp.where(on, rest, 0.0))

    dsend[:, :BLK] = dchunk[...]
    is_p = cg == r

    def pg_copy(i):
        return remote(dsend, pg.at[i], pg_send, pg_recv.at[i], (r, g))

    @pl.when(g != c)
    def _():
        pg_copy(part).start()

    for t in (1, 2):
        for a in range(GR):
            p_copy(a, t).wait_recv()
            tile[a] += p_r[a, t - 1, :, :BLK].astype(F32)

    def gather(i):
        src_c = (c % GR) * NROW + i

        @pl.when(jnp.logical_and(is_p, src_c != c))
        def _():
            pg_copy(i).wait_recv()
            pg_out[i] = pg[i, :, :BLK]

        @pl.when(jnp.logical_and(is_p, src_c == c))
        def _():
            pg_out[i] = dchunk[...]

        @pl.when(jnp.logical_not(is_p))
        def _():
            rows = lax.broadcasted_iota(jnp.int32, (CH, BLK), 0) + i * CH
            cols = lax.broadcasted_iota(jnp.int32, (CH, BLK), 1)
            pg_out[i] = jnp.where(rows == cols, 1.0, 0.0).astype(F32)
    each(0, NROW, gather)

    @pl.when(g != c)
    def _():
        pg_copy(part).wait_send()

    def drain(n):
        for a in range(GR):
            goes, cps = sends(n, a)

            @pl.when(goes)
            def _():
                for cp in cps:
                    cp.wait_send()
        j, cps = term(n)

        @pl.when(j // GR != r)
        def _():
            for cp in cps:
                cp.wait_send()

        @pl.when(n > 0)
        def _():
            row_copy(n).wait_send()
    each(0, NCOL, drain)
    for a in range(GR):
        for cp in relays(a) + [p_copy(a, 1), p_copy(a, 2)]:
            cp.wait_send()


def form(minv, wrow, wcol, cam):
    any_ = pl.BlockSpec(memory_space=pl.ANY)
    vm = pl.BlockSpec(memory_space=pltpu.VMEM)
    dma = pltpu.SemaphoreType.DMA
    legs = SIDE - 1
    return pl.pallas_call(
        form_kernel,
        out_shape=(jax.ShapeDtypeStruct((GR, BLK, BLK), F32), jax.ShapeDtypeStruct((CH, BLK), F32),
                   jax.ShapeDtypeStruct((CH, WIDE), BF16), jax.ShapeDtypeStruct((NROW, CH, BLK), F32)),
        in_specs=[vm] + [any_] * 3,
        out_specs=(vm, vm, vm, vm),
        scratch_shapes=[
            pltpu.VMEM((2, GR * K3, BLK), BF16),
            pltpu.VMEM((2, GR * K3, BLK), BF16),
            pltpu.VMEM((NCOL, GR, K3, WIDE), BF16),
            pltpu.VMEM((GR, SIDE, legs * K3, MAIN), BF16),
            pltpu.VMEM((GR, SIDE, legs * K3, WIDE), BF16),
            pltpu.VMEM((GR, K3, K3), BF16),
            pltpu.VMEM((NCOL, REST, WIDE), BF16),
            pltpu.VMEM((NCOL, CUT, CUT), BF16),
            pltpu.VMEM((NROW, GR, REST, WIDE), BF16),
            pltpu.VMEM((NROW, GR, CUT, CUT), BF16),
            pltpu.VMEM((GR, legs, BLK, WIDE), BF16),
            pltpu.VMEM((GR, 2, BLK, WIDE), BF16),
            pltpu.VMEM((GR, CUT, WIDE), BF16),
            pltpu.VMEM((GR, REST, WIDE), BF16),
            pltpu.VMEM((NCOL, CH, WIDE), BF16),
            pltpu.VMEM((NCOL, CH, WIDE), BF16),
            pltpu.VMEM((NROW, CH, WIDE), F32),
            pltpu.VMEM((CH, BLK), F32),
            pltpu.VMEM((CH, BLK), F32),
            pltpu.VMEM((CH, WIDE), F32),
            dma((2, 2)), dma, dma((GR, NCOL)), dma((GR, SIDE, legs)), dma((GR, NCOL)), dma((GR, SIDE, legs)),
            dma((2, NCOL)), dma((2, NROW, GR)), dma((GR, 2)), dma((GR, 2)), dma((GR, 2)), dma((GR, 2)),
            dma((NCOL,)), dma((NCOL,)), dma, dma((NROW,)),
        ],
        compiler_params=pltpu.CompilerParams(collective_id=0, has_side_effects=True, vmem_limit_bytes=62 * 2**20),
        name="form",
    )(minv, wrow, wcol, cam)


def minv_table(point_inv, pair_counts):
    inv = point_inv.reshape(NCOL, GR, SLOT, 3, 3)
    live = lax.broadcasted_iota(jnp.int32, (NCOL, GR, SLOT), 2) < pair_counts.reshape(NCOL, GR)[:, :, None]
    masked = inv * live[..., None, None].astype(BF16)
    rows = jnp.transpose(masked, (0, 1, 3, 4, 2)).reshape(NCOL, GR, 3, K3)
    return jnp.pad(rows, ((0, 0), (0, 0), (0, 5), (0, 0))).reshape(NCOL, 16, K3)


def stack_rows(jac):
    return jnp.transpose(jac.reshape(jac.shape[2:]), (0, 1, 3, 2, 4)).reshape(NCOL, GR * K3, BLK)


def mm(lhs, rhs):
    return jnp.dot(lhs.astype(BF16), rhs.astype(BF16), preferred_element_type=F32)


def mm_high(lhs, rhs):
    return jnp.dot(lhs, rhs, preferred_element_type=F32, precision=lax.Precision.HIGHEST)


def inverse_kernel(pg, tile, xinv, pmat, tile_out, both, e, y, res, sem, out_sem):
    r = lax.axis_index("row")
    c = lax.axis_index("col")
    is_p = (c // GR == r).astype(F32)
    cp = pltpu.make_async_copy(tile, both, sem)
    keep = pltpu.make_async_copy(both, tile_out, out_sem)
    cp.start()
    rows = lax.broadcasted_iota(jnp.int32, (BLK, BLK), 0)
    cols = lax.broadcasted_iota(jnp.int32, (BLK, BLK), 1)
    eye = jnp.where(rows == cols, 1.0, 0.0).astype(F32)
    cp.wait()
    keep.start()
    wide = 0.5 * pg[...] - both[c % GR] * is_p
    p = wide + wide.T
    pmat[...] = p
    dd = p * eye
    s_row = lax.rsqrt(jnp.sum(dd, axis=0, keepdims=True))
    s_col = lax.rsqrt(jnp.sum(dd, axis=1, keepdims=True))
    b = p * s_row * s_col
    e[...] = eye - b
    e2 = mm(e[...], e[...])
    f2 = jnp.sum(e2 * e2)

    @pl.when(f2 < 0.9)
    def _():
        y[...] = e[...] + e2 + mm(e[...], e2)

    @pl.when(jnp.logical_not(f2 < 0.9))
    def _():
        big = jnp.max(jnp.sum(jnp.abs(eye - e[...]), axis=1, keepdims=True))
        y[...] = eye * (1.0 / big - 1.0)

    def residual(mul):
        out = e[...] - y[...] + mul(y[...], e[...])
        res[...] = out
        return jnp.sum(out * out)

    def more(state):
        step, size = state
        return jnp.logical_and(size > 1.6e-5, step < 64)

    def newton(state):
        step, _ = state

        def low():
            y[...] = y[...] + res[...] + mm(res[...], y[...])
            return residual(mm)

        def high():
            y[...] = y[...] + res[...] + mm_high(res[...], y[...])
            return residual(mm_high)
        return step + 1, lax.cond(step < 6, low, high)
    lax.while_loop(more, newton, (jnp.int32(0), residual(mm)))
    xinv[...] = (eye + y[...]) * s_row * s_col
    keep.wait()


def inverse(pg, tile):
    vm = pl.BlockSpec(memory_space=pltpu.VMEM)
    sq = jax.ShapeDtypeStruct((BLK, BLK), F32)
    return pl.pallas_call(
        inverse_kernel,
        out_shape=(sq, sq, jax.ShapeDtypeStruct((GR, BLK, BLK), F32)),
        in_specs=[vm, pl.BlockSpec(memory_space=pl.ANY)],
        out_specs=(vm, vm, pl.BlockSpec(memory_space=pl.ANY)),
        scratch_shapes=[pltpu.VMEM((GR, BLK, BLK), F32)] + [pltpu.VMEM((BLK, BLK), F32)] * 3 + [pltpu.SemaphoreType.DMA] * 2,
        compiler_params=pltpu.CompilerParams(vmem_limit_bytes=48 * 2**20),
        name="inverse",
    )(pg, tile)


LT = 5
REFINE = 2


def lanes(t):
    return 128 * t, min(128 * (t + 1), BLK)


def spread(mat, vec):
    rows = mat.shape[0]
    acc = jnp.zeros((rows, 128), F32)
    for t in range(LT):
        lo, hi = lanes(t)
        part = mat[:, lo:hi] * vec[t:t + 1, :hi - lo]
        if hi - lo < 128:
            part = jnp.concatenate([part, jnp.zeros((rows, 128 - (hi - lo)), F32)], axis=1)
        acc = acc + part
    return acc


def fold(acc):
    out = []
    for t in range(LT):
        lo, hi = lanes(t)
        blk = acc[lo:hi, :]
        if hi - lo < 128:
            blk = jnp.concatenate([blk, jnp.zeros((128 - (hi - lo), 128), F32)], axis=0)
        out.append(jnp.sum(blk.T, axis=0, keepdims=True))
    return jnp.concatenate(out + [jnp.zeros((8 - LT, 128), F32)], axis=0)


def columns(vec):
    return jnp.concatenate([jnp.broadcast_to(vec[t:t + 1, :], (128, 128)).T for t in range(LT)], axis=0)


def matvec(mat, vec):
    return fold(spread(mat, vec))


def cg_kernel(tile, dchunk, xinv, pmat, rhs, sol, resid,
              zbuf, zsrc, cbuf, csrc, bbuf, bsrc, sbuf, ssrc, fbuf, fsrc, acc, state,
              zr_send, zc_send, z_recv, c_send, b_send, c_recv, b_recv,
              s_send, s_recv, f_send, f_recv):
    r = lax.axis_index("row")
    c = lax.axis_index("col")
    ap = c % GR
    cg = c // GR
    half = c // NROW
    part = c % NROW
    is_p = cg == r
    not_p = jnp.logical_not(is_p)

    barrier = pltpu.get_barrier_semaphore()

    def greet(i, n):
        pl.semaphore_signal(barrier, inc=1, device_id=(r, lax.rem(c + i, NCOL)), device_id_type=MESH)

        @pl.when(i < NROW)
        def _():
            pl.semaphore_signal(barrier, inc=1, device_id=(lax.rem(r + i, NROW), c), device_id_type=MESH)

        @pl.when(is_p)
        def _():
            other = lax.rem(c + i, NCOL)
            pl.semaphore_signal(barrier, inc=1, device_id=(other // GR, other), device_id_type=MESH)
        return n
    lax.fori_loop(1, NCOL, greet, 0)
    pl.semaphore_wait(barrier, NCOL - 1 + NROW - 1 + (NCOL - 1) * is_p.astype(jnp.int32))

    def zr_copy(it, d):
        return remote(zsrc.at[it], zbuf.at[it, ap], zr_send.at[it, d], z_recv.at[it, ap], (r, lax.rem(c + d, NCOL)))

    def zc_copy(it, d):
        return remote(zsrc.at[it], zbuf.at[it, 2], zc_send.at[it, d], z_recv.at[it, 2], (lax.rem(r + d, NROW), c))

    def z_from(it, slot):
        return remote(zsrc.at[it], zbuf.at[it, slot], zr_send.at[it, 0], z_recv.at[it, slot], (lax.rem(r + 1, NROW), c))

    def s_copy(k, d):
        other = lax.rem(c + d, NCOL)
        return remote(ssrc.at[k], sbuf.at[k, c], s_send.at[k, d], s_recv.at[k], (other // GR, other))

    def c_copy(it, a):
        return remote(csrc.at[it, a], cbuf.at[it, c], c_send.at[it, a], c_recv.at[it], (r, GR * r + a))

    def b_copy(it):
        return remote(bsrc.at[it], bbuf.at[it, r], b_send.at[it], b_recv.at[it], (cg, c))

    def take(buf, sem, count):
        pltpu.make_async_copy(buf.at[pl.ds(0, count)], buf.at[pl.ds(0, count)], sem).wait()

    def f_copy(d):
        return remote(fsrc, fbuf.at[ap], f_send.at[d], f_recv.at[ap], (r, lax.rem(c + d, NCOL)))

    def f_from(a):
        return remote(fsrc, fbuf.at[a], f_send.at[0], f_recv.at[a], (r, GR * r + a))

    def exchange(k, top, bottom):
        upper = lax.broadcasted_iota(jnp.int32, (8, 128), 0) < 4
        ssrc[k] = jnp.where(upper, jnp.sum(top), jnp.sum(bottom))
        each(1, NCOL, lambda d: s_copy(k, d).start())

    def totals(k):
        take(sbuf.at[k], s_recv.at[k], NCOL - 1)
        sbuf[k, c] = ssrc[k]
        both = jnp.sum(sbuf[k], axis=0)
        return both[0:1, :], both[4:5, :]

    def apply(vec):
        out = matvec(xinv, vec)
        for _ in range(REFINE):
            out = out + matvec(xinv, vec - matvec(pmat, out))
        return out

    def spread_out(it, vec):
        zsrc[it] = vec
        each(1, NCOL, lambda d: zr_copy(it, d).start())
        each(1, NROW, lambda d: zc_copy(it, d).start())
        zbuf[it, ap] = vec
        zbuf[it, 2] = vec

    def products(it):
        for slot in range(3):
            @pl.when(not_p if slot == 2 else c != GR * r + slot)
            def _():
                z_from(it, slot).wait_recv()

        zc = zbuf[it, 2]
        back = [jnp.zeros((1, hi - lo), F32) for lo, hi in map(lanes, range(LT))]
        for a in range(GR):
            acc[a] = -spread(tile[a], zc)
            zcol = columns(zbuf[it, a])
            for t in range(LT):
                lo, hi = lanes(t)
                back[t] = back[t] + jnp.sum(tile[a, :, lo:hi] * zcol[:BLK, :hi - lo], axis=0, keepdims=True)
        rows = pl.ds(pl.multiple_of(part * CH, 8), CH)
        acc[half, rows, :] += spread(dchunk[...], zbuf[it, half])
        back[LT - 1] = jnp.concatenate([back[LT - 1], jnp.zeros((1, 128 * LT - BLK), F32)], axis=1)
        bsrc[it] = jnp.concatenate(back + [jnp.zeros((8 - LT, 128), F32)], axis=0)

        @pl.when(not_p)
        def _():
            b_copy(it).start()
        for a in range(GR):
            csrc[it, a] = fold(acc[a])

            @pl.when(c != GR * r + a)
            def _():
                c_copy(it, a).start()

    def collect(it):
        take(cbuf.at[it], c_recv.at[it], NCOL - 1)
        take(bbuf.at[it], b_recv.at[it], NROW - 1)
        cbuf[it, c] = csrc[it, ap]
        bbuf[it, r] = bsrc[it]
        return jnp.sum(cbuf[it], axis=0) - jnp.sum(bbuf[it], axis=0)

    @pl.when(is_p)
    def _():
        spread_out(0, apply(rhs[ap]))
    products(0)

    @pl.when(is_p)
    def _():
        image = collect(0)
        state[0] = image
        spread_out(1, apply(image))
        exchange(0, rhs[ap] * zsrc[0], zsrc[0] * image)
    products(1)

    @pl.when(is_p)
    def _():
        first, image = zsrc[0], state[0]
        rz, curve = totals(0)
        alpha = rz / curve
        res = rhs[ap] - alpha * image
        second = first - alpha * zsrc[1]
        exchange(1, res * second, res * second)
        moved = image - alpha * collect(1)
        rz_next, _ = totals(1)
        beta = rz_next / rz
        direction = second + beta * first
        image = moved + beta * image
        exchange(2, direction * image, direction * image)
        curve, _ = totals(2)
        step = rz_next / curve
        fsrc[0] = alpha * first + step * direction
        fsrc[1] = res - step * image
        each(1, NCOL, lambda d: f_copy(d).start())
        fbuf[ap] = fsrc[...]

    for a in range(GR):
        @pl.when(c != GR * r + a)
        def _():
            f_from(a).wait_recv()
        sol[a] = fbuf[a, 0]
        resid[a] = fbuf[a, 1]

    for it in range(ITERS):
        @pl.when(not_p)
        def _():
            b_copy(it).wait_send()
        for a in range(GR):
            @pl.when(c != GR * r + a)
            def _():
                c_copy(it, a).wait_send()

    @pl.when(is_p)
    def _():
        for it in range(ITERS):
            each(1, NCOL, lambda d: zr_copy(it, d).wait_send())
            each(1, NROW, lambda d: zc_copy(it, d).wait_send())
        for k in range(3):
            each(1, NCOL, lambda d: s_copy(k, d).wait_send())
        each(1, NCOL, lambda d: f_copy(d).wait_send())


def gradients(tile, dchunk, xinv, pmat, rhs):
    vm = pl.BlockSpec(memory_space=pltpu.VMEM)
    dma = pltpu.SemaphoreType.DMA
    v = lambda *lead: pltpu.VMEM((*lead, 8, 128), F32)
    vec = jax.ShapeDtypeStruct((GR, 8, 128), F32)
    return pl.pallas_call(
        cg_kernel,
        out_shape=(vec, vec),
        in_specs=[vm] * 5,
        out_specs=(vm, vm),
        scratch_shapes=[
            v(ITERS, 3), v(ITERS), v(ITERS, NCOL), v(ITERS, GR), v(ITERS, NROW), v(ITERS), v(3, NCOL), v(3),
            v(GR, 2), v(2), pltpu.VMEM((GR, BLK, 128), F32), v(1),
            dma((ITERS, NCOL)), dma((ITERS, NROW)), dma((ITERS, 3)),
            dma((ITERS, GR)), dma((ITERS,)), dma((ITERS,)), dma((ITERS,)),
            dma((3, NCOL)), dma((3,)), dma((NCOL,)), dma((GR,)),
        ],
        compiler_params=pltpu.CompilerParams(collective_id=1, has_side_effects=True, vmem_limit_bytes=40 * 2**20),
        name="gradients",
    )(tile, dchunk, xinv, pmat, rhs)


def subtract_kernel(cam, terms, out):
    rows = lax.broadcasted_iota(jnp.int32, (CH, BLK), 0)
    cols = lax.broadcasted_iota(jnp.int32, (CH, BLK), 1)
    for a in range(GR):
        for lo in range(0, BLK, CH):
            part = terms[a, lo:lo + CH, :]
            rest = part[:, BLK:BLK + 1].astype(F32)
            out[a, lo:lo + CH, :] = cam[a, lo:lo + CH, :] - (
                part[:, :BLK].astype(F32) + jnp.where(rows + lo == cols, rest, 0.0))


def subtract(cam, terms):
    vm = pl.BlockSpec(memory_space=pltpu.VMEM)
    return pl.pallas_call(
        subtract_kernel,
        out_shape=jax.ShapeDtypeStruct((GR, BLK, BLK), F32),
        in_specs=[vm, vm],
        out_specs=vm,
        compiler_params=pltpu.CompilerParams(vmem_limit_bytes=24 * 2**20),
        name="subtract",
    )(cam, terms)


def body(jac_row, jac_col, point_inv, pair_counts, camera_blocks, right_side):
    tile, dchunk, terms, pg = form(minv_table(point_inv, pair_counts), stack_rows(jac_row), stack_rows(jac_col),
                                   camera_blocks.reshape(NCOL, CH, BLK))
    xinv, pmat, pairs = inverse(pg.reshape(BLK, BLK), tile)
    wide = 128 * LT
    rhs = jnp.pad(right_side, ((0, 0), (0, wide - BLK))).reshape(GR, LT, 128)
    rhs = jnp.pad(rhs, ((0, 0), (0, 8 - LT), (0, 0)))
    diag = subtract(camera_blocks, lax.all_gather(terms, "col", axis=0, tiled=True).reshape(GR, BLK, WIDE))
    sol, res = gradients(tile, dchunk, xinv, pmat, rhs)
    back = lambda v: v[:, :LT].reshape(GR, wide)[:, :BLK]
    return pairs[:, None], diag, back(sol), back(res)


def solution(mesh):
    return jax.shard_map(
        body,
        mesh=mesh,
        in_specs=(
            P("row", "col", None, None, None, None, None),
            P("row", "col", None, None, None, None, None),
            P("row", "col", None, None, None, None),
            P("row", "col", None, None),
            P("row", None, None),
            P("row", None),
        ),
        out_specs=(
            P("row", "col", None, None),
            P("row", None, None),
            P("row", None),
            P("row", None),
        ),
        check_vma=False,
    )
```

```python
import jax
import jax.numpy as jnp
from jax import lax
from jax.experimental import pallas as pl
from jax.experimental.pallas import tpu as pltpu
from jax.sharding import PartitionSpec as P

MESH = pl.DeviceIdType.MESH
F32 = jnp.float32
BF16 = jnp.bfloat16
NROW, NCOL, GR, SLOT, BLK = 8, 16, 2, 64, 576
SIDE = 4
K3 = 3 * SLOT
CH = 72
WIDE = 640
MAIN = 512
CUT = 256
REST = BLK - CUT
ITERS = 2

OFF = (2, 1, 3, 0)
ORDER = [(u, v) for t in range(SIDE) for u in range(SIDE) for v in range(SIDE) if min(u, v) == t]


def pick(table, n):
    return sum(jnp.where(n == i, value, 0) for i, value in enumerate(table))


def tn(lhs, rhs):
    return lax.dot_general(lhs, rhs, (((0,), (0,)), ((), ())), preferred_element_type=F32)


def each(lo, hi, fn):
    def body(i, n):
        fn(i)
        return n
    lax.fori_loop(lo, hi, body, 0)


def remote(src, dst, ss, rs, dev):
    return pltpu.make_async_remote_copy(src_ref=src, dst_ref=dst, send_sem=ss, recv_sem=rs, device_id=dev,
                                        device_id_type=MESH)


def form_kernel(minv, wrow, wcol, cam, tile, dchunk, terms, pg_out,
                lrow, lcol, limg, rrow, rimg, big, ta_s, tb_s, ta_r, tb_r, p_s, p_r, h0_r, h1_r, srow, qrow, pg, camv, tsum, dsend,
                l_sem, cam_sem, w_send, w_recv, i_send, i_recv, t_send, t_recv, p_send, p_recv, h_send, h_recv,
                rs_send, rs_recv, pg_send, pg_recv):
    r = lax.axis_index("row")
    c = lax.axis_index("col")
    z, x = c // SIDE, lax.rem(c, SIDE)
    cg = c // GR
    g = GR * r + c // NROW
    part = c % NROW

    barrier = pltpu.get_barrier_semaphore()

    def greet(i):
        pl.semaphore_signal(barrier, inc=1, device_id=(r, lax.rem(c + i, NCOL)), device_id_type=MESH)

        @pl.when(i < NROW)
        def _():
            pl.semaphore_signal(barrier, inc=1, device_id=(lax.rem(r + i, NROW), c), device_id_type=MESH)
    each(1, NCOL, greet)

    def at(dz, dx):
        return lax.rem(z + dz, SIDE) * SIDE + lax.rem(x + dx, SIDE)

    def place(n):
        u1, v1 = pick([o[0] for o in ORDER], n), pick([o[1] for o in ORDER], n)
        return u1, v1, pick([OFF[o[0]] for o in ORDER], n), pick([OFF[o[1]] for o in ORDER], n)

    def loads(n):
        _, _, u, v = place(n)
        slot = lax.rem(n, 2)
        return [pltpu.make_async_copy(src.at[at(u, v)], dst.at[slot], l_sem.at[k, slot])
                for k, (src, dst) in enumerate(((wrow, lrow), (wcol, lcol)))]

    def sends(n, a):
        u1, v1, u, v = place(n)
        d, t = (u, v1) if a == 0 else (v, u1)
        dev = (r, at(u, 0) if a == 0 else at(0, v))
        k = jnp.maximum(d - 1, 0)
        rows = pl.ds(K3 * k, K3)
        return d > 0, [
            remote(wrow.at[at(u, v), pl.ds(K3 * a, K3), pl.ds(0, MAIN)], rrow.at[a, t, rows], w_send.at[a, n], w_recv.at[a, t, k], dev),
            remote(limg.at[n, a], rimg.at[a, t, rows], i_send.at[a, n], i_recv.at[a, t, k], dev)]

    def term(n):
        _, _, u, v = place(n)
        j = at(u, v)
        dev = (j // GR, c)
        s = lax.rem(j, GR)
        return j, [remote(ta_s.at[n], ta_r.at[r, s], t_send.at[0, n], t_recv.at[0, r, s], dev),
                   remote(tb_s.at[n], tb_r.at[r, s], t_send.at[1, n], t_recv.at[1, r, s], dev)]

    cam_copy = pltpu.make_async_copy(cam.at[c], camv, cam_sem)
    cam_copy.start()
    for cp in loads(0):
        cp.start()
    tile[...] = jnp.zeros_like(tile)
    for ref in (ta_s, srow):
        ref[:, :, MAIN:] = jnp.zeros((*ref.shape[:2], WIDE - MAIN), BF16)
    for a in range(GR):
        p_s[a, :, :, MAIN:] = jnp.zeros((SIDE - 1, BLK, WIDE - MAIN), BF16)
    dsend[:, MAIN:] = jnp.zeros((CH, WIDE - MAIN), F32)
    row_i = lax.broadcasted_iota(jnp.int32, (SLOT, K3), 0)
    col_i = lax.broadcasted_iota(jnp.int32, (SLOT, K3), 1)
    eye = jnp.where(lax.rem(col_i, SLOT) == row_i, 1.0, 0.0).astype(F32)
    pl.semaphore_wait(barrier, NCOL - 1 + NROW - 1)

    def local(n):
        _, _, u, v = place(n)
        slot = lax.rem(n, 2)

        @pl.when(n + 1 < NCOL)
        def _():
            for cp in loads(n + 1):
                cp.start()
        for a in range(GR):
            goes, cps = sends(n, a)

            @pl.when(goes)
            def _():
                cps[0].start()
        for cp in loads(n):
            cp.wait()
        j = at(u, v)
        top, bot = [], []
        for a in range(GR):
            ent = minv[j, 8 * a:8 * a + 8, :].astype(F32)
            for k in range(3):
                big[a, SLOT * k:SLOT * (k + 1), :] = (eye * ent[k:k + 1, :]).astype(BF16)
            wr = lrow[slot, K3 * a:K3 * (a + 1), :]
            wc = lcol[slot, K3 * a:K3 * (a + 1), :]
            ci = jnp.dot(big[a], wc, preferred_element_type=F32)
            limg[n, a, :, :MAIN] = ci[:, :MAIN].astype(BF16)
            limg[n, a, :, MAIN:] = jnp.concatenate([ci[:, MAIN:], wr[:, MAIN:].astype(F32)], axis=1).astype(BF16)
            goes, cps = sends(n, a)

            @pl.when(goes)
            def _():
                cps[1].start()
            ri = jnp.dot(big[a], wr, preferred_element_type=F32).astype(BF16)
            tile[a, CUT:, :] += tn(wr[:, CUT:], ri)
            tile[a, :CUT, :CUT] += tn(wr[:, :CUT], ri[:, :CUT])
        wc0, wc1 = lcol[slot, :K3, :], lcol[slot, K3:, :]
        ta_s[n, :, :BLK] = (tn(wc0[:, CUT:], limg[n, 0, :, :BLK]) + tn(wc1[:, CUT:], limg[n, 1, :, :BLK])).astype(BF16)
        tb_s[n] = (tn(wc0[:, :CUT], limg[n, 0, :, :CUT]) + tn(wc1[:, :CUT], limg[n, 1, :, :CUT])).astype(BF16)
        _, cps = term(n)

        @pl.when(j // GR != r)
        def _():
            for cp in cps:
                cp.start()

        @pl.when(j // GR == r)
        def _():
            s = lax.rem(j, GR)
            ta_r[r, s] = ta_s[n]
            tb_r[r, s] = tb_s[n]
    each(0, NCOL, local)

    def along(a, off):
        return (r, at(0, off) if a == 0 else at(off, 0))

    def own_rows(a, t):
        j = at(0, OFF[t]) if a == 0 else at(OFF[t], 0)
        return pltpu.make_async_copy(wrow.at[j, pl.ds(K3 * a, K3)], lrow.at[a, pl.ds(0, K3)], l_sem.at[0, a])

    def arrive(a, t):
        for k in range(SIDE - 1):
            rows = pl.ds(K3 * k, K3)
            dev = (r, at(k + 1, 0))
            remote(wrow.at[0, pl.ds(0, K3), pl.ds(0, MAIN)], rrow.at[a, t, rows], w_send.at[a, 0], w_recv.at[a, t, k], dev).wait_recv()
            remote(limg.at[0, a], rimg.at[a, t, rows], i_send.at[a, 0], i_recv.at[a, t, k], dev).wait_recv()

    def partial(a, t, lo, hi):
        own = ORDER.index((SIDE - 1, t) if a == 0 else (t, SIDE - 1))
        own = tn(lrow[a, :K3, lo:hi], limg[own, a, :, :BLK])
        if lo < MAIN:
            return own + tn(rrow[a, t, :, lo:hi], rimg[a, t, :, :BLK])
        return own + tn(rimg[a, t, :, lo:], rimg[a, t, :, :BLK])[hi - lo:, :]

    blocks = ((0, 256), (256, 512), (512, 576))

    def relays(a):
        return [remote(p_s.at[a, 0, pl.ds(0, CUT)], h0_r.at[a], h_send.at[a, 0], h_recv.at[a, 0], along(a, 1)),
                remote(p_s.at[a, 0, pl.ds(CUT, REST)], h1_r.at[a], h_send.at[a, 1], h_recv.at[a, 1], along(a, 3))]

    def p_copy(a, t):
        return remote(p_s.at[a, t], p_r.at[a, t - 1], p_send.at[a, t - 1], p_recv.at[a, t - 1], along(a, OFF[t]))

    def pairs(t):
        for a in range(GR):
            own_rows(a, t).start()
        for a in range(GR):
            own_rows(a, t).wait()
            arrive(a, t)
            if t > 0:
                relays(a)[t - 1].wait_recv()
            for lo, hi in blocks:
                out = partial(a, t, lo, hi)
                if t == 1 and hi <= CUT:
                    out = out + h0_r[a, lo:hi, :BLK].astype(F32)
                if t == 2 and lo >= CUT:
                    out = out + h1_r[a, lo - CUT:hi - CUT, :BLK].astype(F32)
                p_s[a, t, lo:hi, :BLK] = out.astype(BF16)
            for cp in relays(a) if t == 0 else [p_copy(a, t)]:
                cp.start()
    for t in range(SIDE - 1):
        pairs(t)

    def term_sum(i):
        for s in range(GR):
            @pl.when(i != r)
            def _():
                remote(ta_s.at[0], ta_r.at[i, s], t_send.at[0, 0], t_recv.at[0, i, s], (i, c)).wait_recv()
                remote(tb_s.at[0], tb_r.at[i, s], t_send.at[1, 0], t_recv.at[1, i, s], (i, c)).wait_recv()
            tile[s, CUT:, :] += ta_r[i, s, :, :BLK].astype(F32)
            tile[s, :CUT, :CUT] += tb_r[i, s].astype(F32)
    each(0, NROW, term_sum)
    for a in range(GR):
        tile[a, :CUT, CUT:] = tile[a, CUT:, :CUT].T
    for m in range(NCOL):
        a, i = divmod(m, NROW)
        srow[m, :, :BLK] = tile[a, CH * i:CH * (i + 1), :].astype(BF16)

    def row_copy(d):
        j = lax.rem(c + d, NCOL)
        return remote(srow.at[j], qrow.at[d], rs_send.at[d], rs_recv.at[d], (r, j))
    each(1, NCOL, lambda d: row_copy(d).start())

    last = SIDE - 1
    for a in range(GR):
        own_rows(a, last).start()
    for a in range(GR):
        own_rows(a, last).wait()
        arrive(a, last)
        for lo, hi in blocks:
            tile[a, lo:hi, :] = partial(a, last, lo, hi)

    tsum[...] = srow[c, :, :BLK].astype(F32)

    def row_sum(d):
        row_copy(d).wait_recv()
        tsum[...] += qrow[d, :, :BLK].astype(F32)
    each(1, NCOL, row_sum)
    cam_copy.wait()
    total = tsum[...]
    short = total.astype(BF16)
    on = (lax.broadcasted_iota(jnp.int32, (CH, BLK), 0) + part * CH) == lax.broadcasted_iota(jnp.int32, (CH, BLK), 1)
    rest = jnp.sum(jnp.where(on, total - short.astype(F32), 0.0), axis=1, keepdims=True).astype(BF16).astype(F32)
    terms[:, :BLK] = short
    terms[:, BLK:] = jnp.broadcast_to(rest, (CH, WIDE - BLK)).astype(BF16)
    dchunk[...] = camv[...] - (short.astype(F32) + jnp.where(on, rest, 0.0))

    dsend[:, :BLK] = dchunk[...]
    is_p = cg == r

    def pg_copy(i):
        return remote(dsend, pg.at[i], pg_send, pg_recv.at[i], (r, g))

    @pl.when(g != c)
    def _():
        pg_copy(part).start()

    for t in (1, 2):
        for a in range(GR):
            p_copy(a, t).wait_recv()
            tile[a] += p_r[a, t - 1, :, :BLK].astype(F32)

    def gather(i):
        src_c = (c % GR) * NROW + i

        @pl.when(jnp.logical_and(is_p, src_c != c))
        def _():
            pg_copy(i).wait_recv()
            pg_out[i] = pg[i, :, :BLK]

        @pl.when(jnp.logical_and(is_p, src_c == c))
        def _():
            pg_out[i] = dchunk[...]

        @pl.when(jnp.logical_not(is_p))
        def _():
            rows = lax.broadcasted_iota(jnp.int32, (CH, BLK), 0) + i * CH
            cols = lax.broadcasted_iota(jnp.int32, (CH, BLK), 1)
            pg_out[i] = jnp.where(rows == cols, 1.0, 0.0).astype(F32)
    each(0, NROW, gather)

    @pl.when(g != c)
    def _():
        pg_copy(part).wait_send()

    def drain(n):
        for a in range(GR):
            goes, cps = sends(n, a)

            @pl.when(goes)
            def _():
                for cp in cps:
                    cp.wait_send()
        j, cps = term(n)

        @pl.when(j // GR != r)
        def _():
            for cp in cps:
                cp.wait_send()

        @pl.when(n > 0)
        def _():
            row_copy(n).wait_send()
    each(0, NCOL, drain)
    for a in range(GR):
        for cp in relays(a) + [p_copy(a, 1), p_copy(a, 2)]:
            cp.wait_send()


def form(minv, wrow, wcol, cam):
    any_ = pl.BlockSpec(memory_space=pl.ANY)
    vm = pl.BlockSpec(memory_space=pltpu.VMEM)
    dma = pltpu.SemaphoreType.DMA
    legs = SIDE - 1
    return pl.pallas_call(
        form_kernel,
        out_shape=(jax.ShapeDtypeStruct((GR, BLK, BLK), F32), jax.ShapeDtypeStruct((CH, BLK), F32),
                   jax.ShapeDtypeStruct((CH, WIDE), BF16), jax.ShapeDtypeStruct((NROW, CH, BLK), F32)),
        in_specs=[vm] + [any_] * 3,
        out_specs=(vm, vm, vm, vm),
        scratch_shapes=[
            pltpu.VMEM((2, GR * K3, BLK), BF16),
            pltpu.VMEM((2, GR * K3, BLK), BF16),
            pltpu.VMEM((NCOL, GR, K3, WIDE), BF16),
            pltpu.VMEM((GR, SIDE, legs * K3, MAIN), BF16),
            pltpu.VMEM((GR, SIDE, legs * K3, WIDE), BF16),
            pltpu.VMEM((GR, K3, K3), BF16),
            pltpu.VMEM((NCOL, REST, WIDE), BF16),
            pltpu.VMEM((NCOL, CUT, CUT), BF16),
            pltpu.VMEM((NROW, GR, REST, WIDE), BF16),
            pltpu.VMEM((NROW, GR, CUT, CUT), BF16),
            pltpu.VMEM((GR, legs, BLK, WIDE), BF16),
            pltpu.VMEM((GR, 2, BLK, WIDE), BF16),
            pltpu.VMEM((GR, CUT, WIDE), BF16),
            pltpu.VMEM((GR, REST, WIDE), BF16),
            pltpu.VMEM((NCOL, CH, WIDE), BF16),
            pltpu.VMEM((NCOL, CH, WIDE), BF16),
            pltpu.VMEM((NROW, CH, WIDE), F32),
            pltpu.VMEM((CH, BLK), F32),
            pltpu.VMEM((CH, BLK), F32),
            pltpu.VMEM((CH, WIDE), F32),
            dma((2, 2)), dma, dma((GR, NCOL)), dma((GR, SIDE, legs)), dma((GR, NCOL)), dma((GR, SIDE, legs)),
            dma((2, NCOL)), dma((2, NROW, GR)), dma((GR, 2)), dma((GR, 2)), dma((GR, 2)), dma((GR, 2)),
            dma((NCOL,)), dma((NCOL,)), dma, dma((NROW,)),
        ],
        compiler_params=pltpu.CompilerParams(collective_id=0, has_side_effects=True, vmem_limit_bytes=62 * 2**20),
        name="form",
    )(minv, wrow, wcol, cam)


def minv_table(point_inv, pair_counts):
    inv = point_inv.reshape(NCOL, GR, SLOT, 3, 3)
    live = lax.broadcasted_iota(jnp.int32, (NCOL, GR, SLOT), 2) < pair_counts.reshape(NCOL, GR)[:, :, None]
    masked = inv * live[..., None, None].astype(BF16)
    rows = jnp.transpose(masked, (0, 1, 3, 4, 2)).reshape(NCOL, GR, 3, K3)
    return jnp.pad(rows, ((0, 0), (0, 0), (0, 5), (0, 0))).reshape(NCOL, 16, K3)


def stack_rows(jac):
    return jnp.transpose(jac.reshape(jac.shape[2:]), (0, 1, 3, 2, 4)).reshape(NCOL, GR * K3, BLK)


def mm(lhs, rhs):
    return jnp.dot(lhs.astype(BF16), rhs.astype(BF16), preferred_element_type=F32)


def mm_high(lhs, rhs):
    return jnp.dot(lhs, rhs, preferred_element_type=F32, precision=lax.Precision.HIGHEST)


def inverse_kernel(pg, tile, xinv, pmat, tile_out, both, e, y, res, sem, out_sem):
    r = lax.axis_index("row")
    c = lax.axis_index("col")
    is_p = (c // GR == r).astype(F32)
    cp = pltpu.make_async_copy(tile, both, sem)
    keep = pltpu.make_async_copy(both, tile_out, out_sem)
    cp.start()
    rows = lax.broadcasted_iota(jnp.int32, (BLK, BLK), 0)
    cols = lax.broadcasted_iota(jnp.int32, (BLK, BLK), 1)
    eye = jnp.where(rows == cols, 1.0, 0.0).astype(F32)
    cp.wait()
    keep.start()
    wide = 0.5 * pg[...] - both[c % GR] * is_p
    p = wide + wide.T
    pmat[...] = p
    dd = p * eye
    s_row = lax.rsqrt(jnp.sum(dd, axis=0, keepdims=True))
    s_col = lax.rsqrt(jnp.sum(dd, axis=1, keepdims=True))
    b = p * s_row * s_col
    e[...] = eye - b
    e2 = mm(e[...], e[...])
    f2 = jnp.sum(e2 * e2)

    @pl.when(f2 < 0.9)
    def _():
        y[...] = e[...] + e2 + mm(e[...], e2)

    @pl.when(jnp.logical_not(f2 < 0.9))
    def _():
        big = jnp.max(jnp.sum(jnp.abs(eye - e[...]), axis=1, keepdims=True))
        y[...] = eye * (1.0 / big - 1.0)

    def residual(mul):
        out = e[...] - y[...] + mul(y[...], e[...])
        res[...] = out
        return jnp.sum(out * out)

    def more(state):
        step, size = state
        return jnp.logical_and(size > 1.6e-5, step < 64)

    def newton(state):
        step, _ = state

        def low():
            y[...] = y[...] + res[...] + mm(res[...], y[...])
            return residual(mm)

        def high():
            y[...] = y[...] + res[...] + mm_high(res[...], y[...])
            return residual(mm_high)
        return step + 1, lax.cond(step < 6, low, high)
    lax.while_loop(more, newton, (jnp.int32(0), residual(mm)))
    xinv[...] = (eye + y[...]) * s_row * s_col
    keep.wait()


def inverse(pg, tile):
    vm = pl.BlockSpec(memory_space=pltpu.VMEM)
    sq = jax.ShapeDtypeStruct((BLK, BLK), F32)
    return pl.pallas_call(
        inverse_kernel,
        out_shape=(sq, sq, jax.ShapeDtypeStruct((GR, BLK, BLK), F32)),
        in_specs=[vm, pl.BlockSpec(memory_space=pl.ANY)],
        out_specs=(vm, vm, pl.BlockSpec(memory_space=pl.ANY)),
        scratch_shapes=[pltpu.VMEM((GR, BLK, BLK), F32)] + [pltpu.VMEM((BLK, BLK), F32)] * 3 + [pltpu.SemaphoreType.DMA] * 2,
        compiler_params=pltpu.CompilerParams(vmem_limit_bytes=60 * 2**20),
        name="inverse",
    )(pg, tile)


LT = 5
REFINE = 2


def lanes(t):
    return 128 * t, min(128 * (t + 1), BLK)


def spread(mat, vec):
    rows = mat.shape[0]
    acc = jnp.zeros((rows, 128), F32)
    for t in range(LT):
        lo, hi = lanes(t)
        part = mat[:, lo:hi] * vec[t:t + 1, :hi - lo]
        if hi - lo < 128:
            part = jnp.concatenate([part, jnp.zeros((rows, 128 - (hi - lo)), F32)], axis=1)
        acc = acc + part
    return acc


def fold(acc):
    out = []
    for t in range(LT):
        lo, hi = lanes(t)
        blk = acc[lo:hi, :]
        if hi - lo < 128:
            blk = jnp.concatenate([blk, jnp.zeros((128 - (hi - lo), 128), F32)], axis=0)
        out.append(jnp.sum(blk.T, axis=0, keepdims=True))
    return jnp.concatenate(out + [jnp.zeros((8 - LT, 128), F32)], axis=0)


def columns(vec):
    return jnp.concatenate([jnp.broadcast_to(vec[t:t + 1, :], (128, 128)).T for t in range(LT)], axis=0)


def matvec(mat, vec):
    return fold(spread(mat, vec))


def cg_kernel(tile_in, dchunk, xinv_in, pmat_in, rhs, terms, gathered, sol, resid, tile, xinv, pmat,
              zbuf, zsrc, cbuf, csrc, bbuf, bsrc, sbuf, ssrc, fbuf, fsrc, acc, state,
              m_sem, g_loc, g_send, g_recv, zr_send, zc_send, z_recv, c_send, b_send, c_recv, b_recv,
              s_send, s_recv, f_send, f_recv):
    r = lax.axis_index("row")
    c = lax.axis_index("col")
    ap = c % GR
    cg = c // GR
    half = c // NROW
    part = c % NROW
    is_p = cg == r
    not_p = jnp.logical_not(is_p)
    held = [pltpu.make_async_copy(src, dst, m_sem.at[n])
            for n, (src, dst) in enumerate(((tile_in, tile), (xinv_in, xinv), (pmat_in, pmat)))]
    for cp in held:
        cp.start()

    barrier = pltpu.get_barrier_semaphore()

    def greet(i, n):
        pl.semaphore_signal(barrier, inc=1, device_id=(r, lax.rem(c + i, NCOL)), device_id_type=MESH)

        @pl.when(i < NROW)
        def _():
            pl.semaphore_signal(barrier, inc=1, device_id=(lax.rem(r + i, NROW), c), device_id_type=MESH)

        @pl.when(is_p)
        def _():
            other = lax.rem(c + i, NCOL)
            pl.semaphore_signal(barrier, inc=1, device_id=(other // GR, other), device_id_type=MESH)
        return n
    lax.fori_loop(1, NCOL, greet, 0)
    pl.semaphore_wait(barrier, NCOL - 1 + NROW - 1 + (NCOL - 1) * is_p.astype(jnp.int32))
    for cp in held:
        cp.wait()

    z, x = c // SIDE, lax.rem(c, SIDE)
    four = pl.ds(SIDE * z, SIDE)

    def g_copy(d):
        return remote(terms, gathered.at[c], g_send.at[0, d], g_recv.at[0, d], (r, SIDE * z + lax.rem(x + d, SIDE)))

    def g_from(d):
        other = SIDE * z + lax.rem(x + SIDE - d, SIDE)
        return remote(terms, gathered.at[other], g_send.at[0, d], g_recv.at[0, d], (r, other))

    def g_second(d):
        return remote(gathered.at[four], gathered.at[four], g_send.at[1, d], g_recv.at[1, d],
                      (r, SIDE * lax.rem(z + d, SIDE) + x))

    def g_last(d):
        other = SIDE * lax.rem(z + SIDE - d, SIDE)
        there = gathered.at[pl.ds(other, SIDE)]
        return remote(there, there, g_send.at[1, d], g_recv.at[1, d], (r, other + x))

    def pass_on():
        g_own.wait()
        each(1, SIDE, lambda d: g_from(d).wait_recv())
        each(1, SIDE, lambda d: g_second(d).start())

    def zr_copy(it, d):
        return remote(zsrc.at[it], zbuf.at[it, ap], zr_send.at[it, d], z_recv.at[it, ap], (r, lax.rem(c + d, NCOL)))

    def zc_copy(it, d):
        return remote(zsrc.at[it], zbuf.at[it, 2], zc_send.at[it, d], z_recv.at[it, 2], (lax.rem(r + d, NROW), c))

    def z_from(it, slot):
        return remote(zsrc.at[it], zbuf.at[it, slot], zr_send.at[it, 0], z_recv.at[it, slot], (lax.rem(r + 1, NROW), c))

    def s_copy(k, d):
        other = lax.rem(c + d, NCOL)
        return remote(ssrc.at[k], sbuf.at[k, c], s_send.at[k, d], s_recv.at[k], (other // GR, other))

    def c_copy(it, a):
        return remote(csrc.at[it, a], cbuf.at[it, c], c_send.at[it, a], c_recv.at[it], (r, GR * r + a))

    def b_copy(it):
        return remote(bsrc.at[it], bbuf.at[it, r], b_send.at[it], b_recv.at[it], (cg, c))

    def take(buf, sem, count):
        pltpu.make_async_copy(buf.at[pl.ds(0, count)], buf.at[pl.ds(0, count)], sem).wait()

    def f_copy(d):
        return remote(fsrc, fbuf.at[ap], f_send.at[d], f_recv.at[ap], (r, lax.rem(c + d, NCOL)))

    def f_from(a):
        return remote(fsrc, fbuf.at[a], f_send.at[0], f_recv.at[a], (r, GR * r + a))

    def exchange(k, top, bottom):
        upper = lax.broadcasted_iota(jnp.int32, (8, 128), 0) < 4
        ssrc[k] = jnp.where(upper, jnp.sum(top), jnp.sum(bottom))
        each(1, NCOL, lambda d: s_copy(k, d).start())

    def totals(k):
        take(sbuf.at[k], s_recv.at[k], NCOL - 1)
        sbuf[k, c] = ssrc[k]
        both = jnp.sum(sbuf[k], axis=0)
        return both[0:1, :], both[4:5, :]

    def apply(vec):
        out = matvec(xinv, vec)
        for _ in range(REFINE):
            out = out + matvec(xinv, vec - matvec(pmat, out))
        return out

    def spread_out(it, vec):
        zsrc[it] = vec
        each(1, NCOL, lambda d: zr_copy(it, d).start())
        each(1, NROW, lambda d: zc_copy(it, d).start())
        zbuf[it, ap] = vec
        zbuf[it, 2] = vec

    def products(it):
        for slot in range(3):
            @pl.when(not_p if slot == 2 else c != GR * r + slot)
            def _():
                z_from(it, slot).wait_recv()

        zc = zbuf[it, 2]
        back = [jnp.zeros((1, hi - lo), F32) for lo, hi in map(lanes, range(LT))]
        for a in range(GR):
            acc[a] = -spread(tile[a], zc)
            zcol = columns(zbuf[it, a])
            for t in range(LT):
                lo, hi = lanes(t)
                back[t] = back[t] + jnp.sum(tile[a, :, lo:hi] * zcol[:BLK, :hi - lo], axis=0, keepdims=True)
        rows = pl.ds(pl.multiple_of(part * CH, 8), CH)
        acc[half, rows, :] += spread(dchunk[...], zbuf[it, half])
        back[LT - 1] = jnp.concatenate([back[LT - 1], jnp.zeros((1, 128 * LT - BLK), F32)], axis=1)
        bsrc[it] = jnp.concatenate(back + [jnp.zeros((8 - LT, 128), F32)], axis=0)

        @pl.when(not_p)
        def _():
            b_copy(it).start()
        for a in range(GR):
            csrc[it, a] = fold(acc[a])

            @pl.when(c != GR * r + a)
            def _():
                c_copy(it, a).start()

    def collect(it):
        take(cbuf.at[it], c_recv.at[it], NCOL - 1)
        take(bbuf.at[it], b_recv.at[it], NROW - 1)
        cbuf[it, c] = csrc[it, ap]
        bbuf[it, r] = bsrc[it]
        return jnp.sum(cbuf[it], axis=0) - jnp.sum(bbuf[it], axis=0)

    @pl.when(is_p)
    def _():
        spread_out(0, apply(rhs[ap]))
    g_own = pltpu.make_async_copy(terms, gathered.at[c], g_loc)
    g_own.start()
    each(1, SIDE, lambda d: g_copy(d).start())
    products(0)
    pl.when(is_p)(pass_on)

    @pl.when(is_p)
    def _():
        image = collect(0)
        state[0] = image
        spread_out(1, apply(image))
        exchange(0, rhs[ap] * zsrc[0], zsrc[0] * image)
    products(1)

    pl.when(not_p)(pass_on)

    @pl.when(is_p)
    def _():
        first, image = zsrc[0], state[0]
        rz, curve = totals(0)
        alpha = rz / curve
        res = rhs[ap] - alpha * image
        second = first - alpha * zsrc[1]
        exchange(1, res * second, res * second)
        moved = image - alpha * collect(1)
        rz_next, _ = totals(1)
        beta = rz_next / rz
        direction = second + beta * first
        image = moved + beta * image
        exchange(2, direction * image, direction * image)
        curve, _ = totals(2)
        step = rz_next / curve
        fsrc[0] = alpha * first + step * direction
        fsrc[1] = res - step * image
        each(1, NCOL, lambda d: f_copy(d).start())
        fbuf[ap] = fsrc[...]

    for a in range(GR):
        @pl.when(c != GR * r + a)
        def _():
            f_from(a).wait_recv()
        sol[a] = fbuf[a, 0]
        resid[a] = fbuf[a, 1]
    each(1, SIDE, lambda d: g_last(d).wait_recv())
    each(1, SIDE, lambda d: g_copy(d).wait_send())
    each(1, SIDE, lambda d: g_second(d).wait_send())

    for it in range(ITERS):
        @pl.when(not_p)
        def _():
            b_copy(it).wait_send()
        for a in range(GR):
            @pl.when(c != GR * r + a)
            def _():
                c_copy(it, a).wait_send()

    @pl.when(is_p)
    def _():
        for it in range(ITERS):
            each(1, NCOL, lambda d: zr_copy(it, d).wait_send())
            each(1, NROW, lambda d: zc_copy(it, d).wait_send())
        for k in range(3):
            each(1, NCOL, lambda d: s_copy(k, d).wait_send())
        each(1, NCOL, lambda d: f_copy(d).wait_send())


def gradients(tile, dchunk, xinv, pmat, rhs, terms):
    vm = pl.BlockSpec(memory_space=pltpu.VMEM)
    dma = pltpu.SemaphoreType.DMA
    v = lambda *lead: pltpu.VMEM((*lead, 8, 128), F32)
    vec = jax.ShapeDtypeStruct((GR, 8, 128), F32)
    any_ = pl.BlockSpec(memory_space=pl.ANY)
    return pl.pallas_call(
        cg_kernel,
        out_shape=(jax.ShapeDtypeStruct((NCOL, CH, WIDE), BF16), vec, vec),
        in_specs=[any_, vm, any_, any_, vm, vm],
        out_specs=(any_, vm, vm),
        scratch_shapes=[
            pltpu.VMEM((GR, BLK, BLK), F32), pltpu.VMEM((BLK, BLK), F32), pltpu.VMEM((BLK, BLK), F32),
            v(ITERS, 3), v(ITERS), v(ITERS, NCOL), v(ITERS, GR), v(ITERS, NROW), v(ITERS), v(3, NCOL), v(3),
            v(GR, 2), v(2), pltpu.VMEM((GR, BLK, 128), F32), v(1),
            dma((3,)), dma, dma((2, SIDE)), dma((2, SIDE)), dma((ITERS, NCOL)), dma((ITERS, NROW)), dma((ITERS, 3)),
            dma((ITERS, GR)), dma((ITERS,)), dma((ITERS,)), dma((ITERS,)),
            dma((3, NCOL)), dma((3,)), dma((NCOL,)), dma((GR,)),
        ],
        compiler_params=pltpu.CompilerParams(collective_id=1, has_side_effects=True, vmem_limit_bytes=60 * 2**20),
        name="gradients",
    )(tile, dchunk, xinv, pmat, rhs, terms)


def subtract_kernel(cam, terms, out):
    rows = lax.broadcasted_iota(jnp.int32, (CH, BLK), 0)
    cols = lax.broadcasted_iota(jnp.int32, (CH, BLK), 1)
    for a in range(GR):
        for lo in range(0, BLK, CH):
            part = terms[a, lo:lo + CH, :]
            rest = part[:, BLK:BLK + 1].astype(F32)
            out[a, lo:lo + CH, :] = cam[a, lo:lo + CH, :] - (
                part[:, :BLK].astype(F32) + jnp.where(rows + lo == cols, rest, 0.0))


def subtract(cam, terms):
    vm = pl.BlockSpec(memory_space=pltpu.VMEM)
    return pl.pallas_call(
        subtract_kernel,
        out_shape=jax.ShapeDtypeStruct((GR, BLK, BLK), F32),
        in_specs=[vm, vm],
        out_specs=vm,
        compiler_params=pltpu.CompilerParams(vmem_limit_bytes=24 * 2**20),
        name="subtract",
    )(cam, terms)


def body(jac_row, jac_col, point_inv, pair_counts, camera_blocks, right_side):
    tile, dchunk, terms, pg = form(minv_table(point_inv, pair_counts), stack_rows(jac_row), stack_rows(jac_col),
                                   camera_blocks.reshape(NCOL, CH, BLK))
    xinv, pmat, pairs = inverse(pg.reshape(BLK, BLK), tile)
    wide = 128 * LT
    rhs = jnp.pad(right_side, ((0, 0), (0, wide - BLK))).reshape(GR, LT, 128)
    rhs = jnp.pad(rhs, ((0, 0), (0, 8 - LT), (0, 0)))
    gathered, sol, res = gradients(tile, dchunk, xinv, pmat, rhs, terms)
    diag = subtract(camera_blocks, gathered.reshape(GR, BLK, WIDE))
    back = lambda v: v[:, :LT].reshape(GR, wide)[:, :BLK]
    return pairs[:, None], diag, back(sol), back(res)


def solution(mesh):
    return jax.shard_map(
        body,
        mesh=mesh,
        in_specs=(
            P("row", "col", None, None, None, None, None),
            P("row", "col", None, None, None, None, None),
            P("row", "col", None, None, None, None),
            P("row", "col", None, None),
            P("row", None, None),
            P("row", None),
        ),
        out_specs=(
            P("row", "col", None, None),
            P("row", None, None),
            P("row", None),
            P("row", None),
        ),
        check_vma=False,
    )
```

```python
import jax
import jax.numpy as jnp
from jax import lax
from jax.experimental import pallas as pl
from jax.experimental.pallas import tpu as pltpu
from jax.sharding import PartitionSpec as P

MESH = pl.DeviceIdType.MESH
F32 = jnp.float32
BF16 = jnp.bfloat16
NROW, NCOL, GR, SLOT, BLK = 8, 16, 2, 64, 576
SIDE = 4
K3 = 3 * SLOT
CH = 72
WIDE = 640
MAIN = 512
CUT = 256
REST = BLK - CUT
ITERS = 2

OFF = (2, 1, 3, 0)
ORDER = [(u, v) for t in range(SIDE) for u in range(SIDE) for v in range(SIDE) if min(u, v) == t]


def pick(table, n):
    return sum(jnp.where(n == i, value, 0) for i, value in enumerate(table))


def tn(lhs, rhs):
    return lax.dot_general(lhs, rhs, (((0,), (0,)), ((), ())), preferred_element_type=F32)


def each(lo, hi, fn):
    def body(i, n):
        fn(i)
        return n
    lax.fori_loop(lo, hi, body, 0)


def remote(src, dst, ss, rs, dev):
    return pltpu.make_async_remote_copy(src_ref=src, dst_ref=dst, send_sem=ss, recv_sem=rs, device_id=dev,
                                        device_id_type=MESH)


def form_kernel(minv, wrow, wcol, cam, tile, dchunk, terms, pg_out,
                lrow, lcol, limg, rrow, rimg, big, ta_s, tb_s, ta_r, tb_r, p_s, p_r, h0_r, h1_r, srow, qrow, pg, camv, tsum, dsend,
                l_sem, cam_sem, w_send, w_recv, i_send, i_recv, t_send, t_recv, p_send, p_recv, h_send, h_recv,
                rs_send, rs_recv, pg_send, pg_recv):
    r = lax.axis_index("row")
    c = lax.axis_index("col")
    z, x = c // SIDE, lax.rem(c, SIDE)
    cg = c // GR
    g = GR * r + c // NROW
    part = c % NROW

    barrier = pltpu.get_barrier_semaphore()

    def greet(i):
        pl.semaphore_signal(barrier, inc=1, device_id=(r, lax.rem(c + i, NCOL)), device_id_type=MESH)

        @pl.when(i < NROW)
        def _():
            pl.semaphore_signal(barrier, inc=1, device_id=(lax.rem(r + i, NROW), c), device_id_type=MESH)
    each(1, NCOL, greet)

    def at(dz, dx):
        return lax.rem(z + dz, SIDE) * SIDE + lax.rem(x + dx, SIDE)

    def place(n):
        u1, v1 = pick([o[0] for o in ORDER], n), pick([o[1] for o in ORDER], n)
        return u1, v1, pick([OFF[o[0]] for o in ORDER], n), pick([OFF[o[1]] for o in ORDER], n)

    def loads(n):
        _, _, u, v = place(n)
        slot = lax.rem(n, 2)
        return [pltpu.make_async_copy(src.at[at(u, v)], dst.at[slot], l_sem.at[k, slot])
                for k, (src, dst) in enumerate(((wrow, lrow), (wcol, lcol)))]

    def sends(n, a):
        u1, v1, u, v = place(n)
        d, t = (u, v1) if a == 0 else (v, u1)
        dev = (r, at(u, 0) if a == 0 else at(0, v))
        k = jnp.maximum(d - 1, 0)
        rows = pl.ds(K3 * k, K3)
        return d > 0, [
            remote(wrow.at[at(u, v), pl.ds(K3 * a, K3), pl.ds(0, MAIN)], rrow.at[a, t, rows], w_send.at[a, n], w_recv.at[a, t, k], dev),
            remote(limg.at[n, a], rimg.at[a, t, rows], i_send.at[a, n], i_recv.at[a, t, k], dev)]

    def term(n):
        _, _, u, v = place(n)
        j = at(u, v)
        dev = (j // GR, c)
        s = lax.rem(j, GR)
        return j, [remote(ta_s.at[n], ta_r.at[r, s], t_send.at[0, n], t_recv.at[0, r, s], dev),
                   remote(tb_s.at[n], tb_r.at[r, s], t_send.at[1, n], t_recv.at[1, r, s], dev)]

    cam_copy = pltpu.make_async_copy(cam.at[c], camv, cam_sem)
    cam_copy.start()
    for cp in loads(0):
        cp.start()
    tile[...] = jnp.zeros_like(tile)
    for ref in (ta_s, srow):
        ref[:, :, MAIN:] = jnp.zeros((*ref.shape[:2], WIDE - MAIN), BF16)
    for a in range(GR):
        p_s[a, :, :, MAIN:] = jnp.zeros((SIDE - 1, BLK, WIDE - MAIN), BF16)
    dsend[:, MAIN:] = jnp.zeros((CH, WIDE - MAIN), F32)
    row_i = lax.broadcasted_iota(jnp.int32, (SLOT, K3), 0)
    col_i = lax.broadcasted_iota(jnp.int32, (SLOT, K3), 1)
    eye = jnp.where(lax.rem(col_i, SLOT) == row_i, 1.0, 0.0).astype(F32)
    pl.semaphore_wait(barrier, NCOL - 1 + NROW - 1)

    def local(n):
        _, _, u, v = place(n)
        slot = lax.rem(n, 2)

        @pl.when(n + 1 < NCOL)
        def _():
            for cp in loads(n + 1):
                cp.start()
        for a in range(GR):
            goes, cps = sends(n, a)

            @pl.when(goes)
            def _():
                cps[0].start()
        for cp in loads(n):
            cp.wait()
        j = at(u, v)
        top, bot = [], []
        for a in range(GR):
            ent = minv[j, 8 * a:8 * a + 8, :].astype(F32)
            for k in range(3):
                big[a, SLOT * k:SLOT * (k + 1), :] = (eye * ent[k:k + 1, :]).astype(BF16)
            wr = lrow[slot, K3 * a:K3 * (a + 1), :]
            wc = lcol[slot, K3 * a:K3 * (a + 1), :]
            ci = jnp.dot(big[a], wc, preferred_element_type=F32)
            limg[n, a, :, :MAIN] = ci[:, :MAIN].astype(BF16)
            limg[n, a, :, MAIN:] = jnp.concatenate([ci[:, MAIN:], wr[:, MAIN:].astype(F32)], axis=1).astype(BF16)
            goes, cps = sends(n, a)

            @pl.when(goes)
            def _():
                cps[1].start()
            ri = jnp.dot(big[a], wr, preferred_element_type=F32).astype(BF16)
            tile[a, CUT:, :] += tn(wr[:, CUT:], ri)
            tile[a, :CUT, :CUT] += tn(wr[:, :CUT], ri[:, :CUT])
        wc0, wc1 = lcol[slot, :K3, :], lcol[slot, K3:, :]
        ta_s[n, :, :BLK] = (tn(wc0[:, CUT:], limg[n, 0, :, :BLK]) + tn(wc1[:, CUT:], limg[n, 1, :, :BLK])).astype(BF16)
        tb_s[n] = (tn(wc0[:, :CUT], limg[n, 0, :, :CUT]) + tn(wc1[:, :CUT], limg[n, 1, :, :CUT])).astype(BF16)
        _, cps = term(n)

        @pl.when(j // GR != r)
        def _():
            for cp in cps:
                cp.start()

        @pl.when(j // GR == r)
        def _():
            s = lax.rem(j, GR)
            ta_r[r, s] = ta_s[n]
            tb_r[r, s] = tb_s[n]
    each(0, NCOL, local)

    def along(a, off):
        return (r, at(0, off) if a == 0 else at(off, 0))

    def own_rows(a, t):
        j = at(0, OFF[t]) if a == 0 else at(OFF[t], 0)
        return pltpu.make_async_copy(wrow.at[j, pl.ds(K3 * a, K3)], lrow.at[a, pl.ds(0, K3)], l_sem.at[0, a])

    def arrive(a, t):
        for k in range(SIDE - 1):
            rows = pl.ds(K3 * k, K3)
            dev = (r, at(k + 1, 0))
            remote(wrow.at[0, pl.ds(0, K3), pl.ds(0, MAIN)], rrow.at[a, t, rows], w_send.at[a, 0], w_recv.at[a, t, k], dev).wait_recv()
            remote(limg.at[0, a], rimg.at[a, t, rows], i_send.at[a, 0], i_recv.at[a, t, k], dev).wait_recv()

    def partial(a, t, lo, hi):
        own = ORDER.index((SIDE - 1, t) if a == 0 else (t, SIDE - 1))
        own = tn(lrow[a, :K3, lo:hi], limg[own, a, :, :BLK])
        if lo < MAIN:
            return own + tn(rrow[a, t, :, lo:hi], rimg[a, t, :, :BLK])
        return own + tn(rimg[a, t, :, lo:], rimg[a, t, :, :BLK])[hi - lo:, :]

    blocks = ((0, 256), (256, 512), (512, 576))

    def relays(a):
        return [remote(p_s.at[a, 0, pl.ds(0, CUT)], h0_r.at[a], h_send.at[a, 0], h_recv.at[a, 0], along(a, 1)),
                remote(p_s.at[a, 0, pl.ds(CUT, REST)], h1_r.at[a], h_send.at[a, 1], h_recv.at[a, 1], along(a, 3))]

    def p_copy(a, t):
        return remote(p_s.at[a, t], p_r.at[a, t - 1], p_send.at[a, t - 1], p_recv.at[a, t - 1], along(a, OFF[t]))

    def pairs(t):
        for a in range(GR):
            own_rows(a, t).start()
        for a in range(GR):
            own_rows(a, t).wait()
            arrive(a, t)
            if t > 0:
                relays(a)[t - 1].wait_recv()
            for lo, hi in blocks:
                out = partial(a, t, lo, hi)
                if t == 1 and hi <= CUT:
                    out = out + h0_r[a, lo:hi, :BLK].astype(F32)
                if t == 2 and lo >= CUT:
                    out = out + h1_r[a, lo - CUT:hi - CUT, :BLK].astype(F32)
                p_s[a, t, lo:hi, :BLK] = out.astype(BF16)
            for cp in relays(a) if t == 0 else [p_copy(a, t)]:
                cp.start()
    for t in range(SIDE - 1):
        pairs(t)

    def term_sum(i):
        for s in range(GR):
            @pl.when(i != r)
            def _():
                remote(ta_s.at[0], ta_r.at[i, s], t_send.at[0, 0], t_recv.at[0, i, s], (i, c)).wait_recv()
                remote(tb_s.at[0], tb_r.at[i, s], t_send.at[1, 0], t_recv.at[1, i, s], (i, c)).wait_recv()
    each(0, NROW, term_sum)
    for s in range(GR):
        for lo in range(0, REST, SLOT):
            out = tile[s, CUT + lo:CUT + lo + SLOT, :]
            for i in range(NROW):
                out = out + ta_r[i, s, lo:lo + SLOT, :BLK].astype(F32)
            tile[s, CUT + lo:CUT + lo + SLOT, :] = out
        for lo in range(0, CUT, SLOT):
            out = tile[s, lo:lo + SLOT, :CUT]
            for i in range(NROW):
                out = out + tb_r[i, s, lo:lo + SLOT, :].astype(F32)
            tile[s, lo:lo + SLOT, :CUT] = out
    for a in range(GR):
        tile[a, :CUT, CUT:] = tile[a, CUT:, :CUT].T
    for m in range(NCOL):
        a, i = divmod(m, NROW)
        srow[m, :, :BLK] = tile[a, CH * i:CH * (i + 1), :].astype(BF16)

    def row_copy(d):
        j = lax.rem(c + d, NCOL)
        return remote(srow.at[j], qrow.at[d], rs_send.at[d], rs_recv.at[d], (r, j))
    each(1, NCOL, lambda d: row_copy(d).start())

    last = SIDE - 1
    for a in range(GR):
        own_rows(a, last).start()
    for a in range(GR):
        own_rows(a, last).wait()
        arrive(a, last)
        for lo, hi in blocks:
            tile[a, lo:hi, :] = partial(a, last, lo, hi)

    tsum[...] = srow[c, :, :BLK].astype(F32)

    def row_sum(d):
        row_copy(d).wait_recv()
        tsum[...] += qrow[d, :, :BLK].astype(F32)
    each(1, NCOL, row_sum)
    cam_copy.wait()
    total = tsum[...]
    short = total.astype(BF16)
    on = (lax.broadcasted_iota(jnp.int32, (CH, BLK), 0) + part * CH) == lax.broadcasted_iota(jnp.int32, (CH, BLK), 1)
    rest = jnp.sum(jnp.where(on, total - short.astype(F32), 0.0), axis=1, keepdims=True).astype(BF16).astype(F32)
    terms[:, :BLK] = short
    terms[:, BLK:] = jnp.broadcast_to(rest, (CH, WIDE - BLK)).astype(BF16)
    dchunk[...] = camv[...] - (short.astype(F32) + jnp.where(on, rest, 0.0))

    dsend[:, :BLK] = dchunk[...]
    is_p = cg == r

    def pg_copy(i):
        return remote(dsend, pg.at[i], pg_send, pg_recv.at[i], (r, g))

    @pl.when(g != c)
    def _():
        pg_copy(part).start()

    for t in (1, 2):
        for a in range(GR):
            p_copy(a, t).wait_recv()
            tile[a] += p_r[a, t - 1, :, :BLK].astype(F32)

    def gather(i):
        src_c = (c % GR) * NROW + i

        @pl.when(jnp.logical_and(is_p, src_c != c))
        def _():
            pg_copy(i).wait_recv()
            pg_out[i] = pg[i, :, :BLK]

        @pl.when(jnp.logical_and(is_p, src_c == c))
        def _():
            pg_out[i] = dchunk[...]

        @pl.when(jnp.logical_not(is_p))
        def _():
            rows = lax.broadcasted_iota(jnp.int32, (CH, BLK), 0) + i * CH
            cols = lax.broadcasted_iota(jnp.int32, (CH, BLK), 1)
            pg_out[i] = jnp.where(rows == cols, 1.0, 0.0).astype(F32)
    each(0, NROW, gather)

    @pl.when(g != c)
    def _():
        pg_copy(part).wait_send()

    def drain(n):
        for a in range(GR):
            goes, cps = sends(n, a)

            @pl.when(goes)
            def _():
                for cp in cps:
                    cp.wait_send()
        j, cps = term(n)

        @pl.when(j // GR != r)
        def _():
            for cp in cps:
                cp.wait_send()

        @pl.when(n > 0)
        def _():
            row_copy(n).wait_send()
    each(0, NCOL, drain)
    for a in range(GR):
        for cp in relays(a) + [p_copy(a, 1), p_copy(a, 2)]:
            cp.wait_send()


def form(minv, wrow, wcol, cam):
    any_ = pl.BlockSpec(memory_space=pl.ANY)
    vm = pl.BlockSpec(memory_space=pltpu.VMEM)
    dma = pltpu.SemaphoreType.DMA
    legs = SIDE - 1
    return pl.pallas_call(
        form_kernel,
        out_shape=(jax.ShapeDtypeStruct((GR, BLK, BLK), F32), jax.ShapeDtypeStruct((CH, BLK), F32),
                   jax.ShapeDtypeStruct((CH, WIDE), BF16), jax.ShapeDtypeStruct((NROW, CH, BLK), F32)),
        in_specs=[vm] + [any_] * 3,
        out_specs=(vm, vm, vm, vm),
        scratch_shapes=[
            pltpu.VMEM((2, GR * K3, BLK), BF16),
            pltpu.VMEM((2, GR * K3, BLK), BF16),
            pltpu.VMEM((NCOL, GR, K3, WIDE), BF16),
            pltpu.VMEM((GR, SIDE, legs * K3, MAIN), BF16),
            pltpu.VMEM((GR, SIDE, legs * K3, WIDE), BF16),
            pltpu.VMEM((GR, K3, K3), BF16),
            pltpu.VMEM((NCOL, REST, WIDE), BF16),
            pltpu.VMEM((NCOL, CUT, CUT), BF16),
            pltpu.VMEM((NROW, GR, REST, WIDE), BF16),
            pltpu.VMEM((NROW, GR, CUT, CUT), BF16),
            pltpu.VMEM((GR, legs, BLK, WIDE), BF16),
            pltpu.VMEM((GR, 2, BLK, WIDE), BF16),
            pltpu.VMEM((GR, CUT, WIDE), BF16),
            pltpu.VMEM((GR, REST, WIDE), BF16),
            pltpu.VMEM((NCOL, CH, WIDE), BF16),
            pltpu.VMEM((NCOL, CH, WIDE), BF16),
            pltpu.VMEM((NROW, CH, WIDE), F32),
            pltpu.VMEM((CH, BLK), F32),
            pltpu.VMEM((CH, BLK), F32),
            pltpu.VMEM((CH, WIDE), F32),
            dma((2, 2)), dma, dma((GR, NCOL)), dma((GR, SIDE, legs)), dma((GR, NCOL)), dma((GR, SIDE, legs)),
            dma((2, NCOL)), dma((2, NROW, GR)), dma((GR, 2)), dma((GR, 2)), dma((GR, 2)), dma((GR, 2)),
            dma((NCOL,)), dma((NCOL,)), dma, dma((NROW,)),
        ],
        compiler_params=pltpu.CompilerParams(collective_id=0, has_side_effects=True, vmem_limit_bytes=62 * 2**20),
        name="form",
    )(minv, wrow, wcol, cam)


def minv_table(point_inv, pair_counts):
    inv = point_inv.reshape(NCOL, GR, SLOT, 3, 3)
    live = lax.broadcasted_iota(jnp.int32, (NCOL, GR, SLOT), 2) < pair_counts.reshape(NCOL, GR)[:, :, None]
    masked = inv * live[..., None, None].astype(BF16)
    rows = jnp.transpose(masked, (0, 1, 3, 4, 2)).reshape(NCOL, GR, 3, K3)
    return jnp.pad(rows, ((0, 0), (0, 0), (0, 5), (0, 0))).reshape(NCOL, 16, K3)


def stack_rows(jac):
    return jnp.transpose(jac.reshape(jac.shape[2:]), (0, 1, 3, 2, 4)).reshape(NCOL, GR * K3, BLK)


def mm(lhs, rhs):
    return jnp.dot(lhs.astype(BF16), rhs.astype(BF16), preferred_element_type=F32)


def mm_high(lhs, rhs):
    return jnp.dot(lhs, rhs, preferred_element_type=F32, precision=lax.Precision.HIGHEST)


def inverse_kernel(pg, tile, xinv, pmat, tile_out, both, e, y, res, sem, out_sem):
    r = lax.axis_index("row")
    c = lax.axis_index("col")
    is_p = (c // GR == r).astype(F32)
    cp = pltpu.make_async_copy(tile, both, sem)
    keep = pltpu.make_async_copy(both, tile_out, out_sem)
    cp.start()
    rows = lax.broadcasted_iota(jnp.int32, (BLK, BLK), 0)
    cols = lax.broadcasted_iota(jnp.int32, (BLK, BLK), 1)
    eye = jnp.where(rows == cols, 1.0, 0.0).astype(F32)
    cp.wait()
    keep.start()
    wide = 0.5 * pg[...] - both[c % GR] * is_p
    p = wide + wide.T
    pmat[...] = p
    dd = p * eye
    s_row = lax.rsqrt(jnp.sum(dd, axis=0, keepdims=True))
    s_col = lax.rsqrt(jnp.sum(dd, axis=1, keepdims=True))
    b = p * s_row * s_col
    e[...] = eye - b
    e2 = mm(e[...], e[...])
    f2 = jnp.sum(e2 * e2)

    @pl.when(f2 < 0.9)
    def _():
        y[...] = e[...] + e2 + mm(e[...], e2)

    @pl.when(jnp.logical_not(f2 < 0.9))
    def _():
        big = jnp.max(jnp.sum(jnp.abs(eye - e[...]), axis=1, keepdims=True))
        y[...] = eye * (1.0 / big - 1.0)

    def residual(mul):
        out = e[...] - y[...] + mul(y[...], e[...])
        res[...] = out
        return jnp.sum(out * out)

    def more(state):
        step, size = state
        return jnp.logical_and(size > 1.6e-5, step < 64)

    def newton(state):
        step, _ = state

        def low():
            y[...] = y[...] + res[...] + mm(res[...], y[...])
            return residual(mm)

        def high():
            y[...] = y[...] + res[...] + mm_high(res[...], y[...])
            return residual(mm_high)
        return step + 1, lax.cond(step < 6, low, high)
    lax.while_loop(more, newton, (jnp.int32(0), residual(mm)))
    xinv[...] = (eye + y[...]) * s_row * s_col
    keep.wait()


def inverse(pg, tile):
    vm = pl.BlockSpec(memory_space=pltpu.VMEM)
    sq = jax.ShapeDtypeStruct((BLK, BLK), F32)
    return pl.pallas_call(
        inverse_kernel,
        out_shape=(sq, sq, jax.ShapeDtypeStruct((GR, BLK, BLK), F32)),
        in_specs=[vm, pl.BlockSpec(memory_space=pl.ANY)],
        out_specs=(vm, vm, pl.BlockSpec(memory_space=pl.ANY)),
        scratch_shapes=[pltpu.VMEM((GR, BLK, BLK), F32)] + [pltpu.VMEM((BLK, BLK), F32)] * 3 + [pltpu.SemaphoreType.DMA] * 2,
        compiler_params=pltpu.CompilerParams(vmem_limit_bytes=60 * 2**20),
        name="inverse",
    )(pg, tile)


LT = 5
REFINE = 2


def lanes(t):
    return 128 * t, min(128 * (t + 1), BLK)


def spread(mat, vec):
    rows = mat.shape[0]
    acc = jnp.zeros((rows, 128), F32)
    for t in range(LT):
        lo, hi = lanes(t)
        part = mat[:, lo:hi] * vec[t:t + 1, :hi - lo]
        if hi - lo < 128:
            part = jnp.concatenate([part, jnp.zeros((rows, 128 - (hi - lo)), F32)], axis=1)
        acc = acc + part
    return acc


def fold(acc):
    out = []
    for t in range(LT):
        lo, hi = lanes(t)
        blk = acc[lo:hi, :]
        if hi - lo < 128:
            blk = jnp.concatenate([blk, jnp.zeros((128 - (hi - lo), 128), F32)], axis=0)
        out.append(jnp.sum(blk.T, axis=0, keepdims=True))
    return jnp.concatenate(out + [jnp.zeros((8 - LT, 128), F32)], axis=0)


def columns(vec):
    return jnp.concatenate([jnp.broadcast_to(vec[t:t + 1, :], (128, 128)).T for t in range(LT)], axis=0)


def matvec(mat, vec):
    return fold(spread(mat, vec))


def cg_kernel(tile_in, dchunk, xinv_in, pmat_in, rhs, terms, gathered, sol, resid, tile, xinv, pmat,
              zbuf, zsrc, cbuf, csrc, bbuf, bsrc, sbuf, ssrc, fbuf, fsrc, acc, state,
              m_sem, g_loc, g_send, g_recv, zr_send, zc_send, z_recv, c_send, b_send, c_recv, b_recv,
              s_send, s_recv, f_send, f_recv):
    r = lax.axis_index("row")
    c = lax.axis_index("col")
    ap = c % GR
    cg = c // GR
    half = c // NROW
    part = c % NROW
    is_p = cg == r
    not_p = jnp.logical_not(is_p)
    held = [pltpu.make_async_copy(src, dst, m_sem.at[n])
            for n, (src, dst) in enumerate(((tile_in, tile), (xinv_in, xinv), (pmat_in, pmat)))]
    for cp in held:
        cp.start()

    barrier = pltpu.get_barrier_semaphore()

    def greet(i, n):
        pl.semaphore_signal(barrier, inc=1, device_id=(r, lax.rem(c + i, NCOL)), device_id_type=MESH)

        @pl.when(i < NROW)
        def _():
            pl.semaphore_signal(barrier, inc=1, device_id=(lax.rem(r + i, NROW), c), device_id_type=MESH)

        @pl.when(is_p)
        def _():
            other = lax.rem(c + i, NCOL)
            pl.semaphore_signal(barrier, inc=1, device_id=(other // GR, other), device_id_type=MESH)
        return n
    lax.fori_loop(1, NCOL, greet, 0)
    pl.semaphore_wait(barrier, NCOL - 1 + NROW - 1 + (NCOL - 1) * is_p.astype(jnp.int32))
    for cp in held:
        cp.wait()

    z, x = c // SIDE, lax.rem(c, SIDE)
    four = pl.ds(SIDE * z, SIDE)

    def g_copy(d):
        return remote(terms, gathered.at[c], g_send.at[0, d], g_recv.at[0, d], (r, SIDE * z + lax.rem(x + d, SIDE)))

    def g_from(d):
        other = SIDE * z + lax.rem(x + SIDE - d, SIDE)
        return remote(terms, gathered.at[other], g_send.at[0, d], g_recv.at[0, d], (r, other))

    def g_second(d):
        return remote(gathered.at[four], gathered.at[four], g_send.at[1, d], g_recv.at[1, d],
                      (r, SIDE * lax.rem(z + d, SIDE) + x))

    def g_last(d):
        other = SIDE * lax.rem(z + SIDE - d, SIDE)
        there = gathered.at[pl.ds(other, SIDE)]
        return remote(there, there, g_send.at[1, d], g_recv.at[1, d], (r, other + x))

    def pass_on():
        g_own.wait()
        each(1, SIDE, lambda d: g_from(d).wait_recv())
        each(1, SIDE, lambda d: g_second(d).start())

    def zr_copy(it, d):
        return remote(zsrc.at[it], zbuf.at[it, ap], zr_send.at[it, d], z_recv.at[it, ap], (r, lax.rem(c + d, NCOL)))

    def zc_copy(it, d):
        return remote(zsrc.at[it], zbuf.at[it, 2], zc_send.at[it, d], z_recv.at[it, 2], (lax.rem(r + d, NROW), c))

    def z_from(it, slot):
        return remote(zsrc.at[it], zbuf.at[it, slot], zr_send.at[it, 0], z_recv.at[it, slot], (lax.rem(r + 1, NROW), c))

    def s_copy(k, d):
        other = lax.rem(c + d, NCOL)
        return remote(ssrc.at[k], sbuf.at[k, c], s_send.at[k, d], s_recv.at[k], (other // GR, other))

    def c_copy(it, a):
        return remote(csrc.at[it, a], cbuf.at[it, c], c_send.at[it, a], c_recv.at[it], (r, GR * r + a))

    def b_copy(it):
        return remote(bsrc.at[it], bbuf.at[it, r], b_send.at[it], b_recv.at[it], (cg, c))

    def take(buf, sem, count):
        pltpu.make_async_copy(buf.at[pl.ds(0, count)], buf.at[pl.ds(0, count)], sem).wait()

    def f_copy(d):
        return remote(fsrc, fbuf.at[ap], f_send.at[d], f_recv.at[ap], (r, lax.rem(c + d, NCOL)))

    def f_from(a):
        return remote(fsrc, fbuf.at[a], f_send.at[0], f_recv.at[a], (r, GR * r + a))

    def exchange(k, top, bottom):
        upper = lax.broadcasted_iota(jnp.int32, (8, 128), 0) < 4
        ssrc[k] = jnp.where(upper, jnp.sum(top), jnp.sum(bottom))
        each(1, NCOL, lambda d: s_copy(k, d).start())

    def totals(k):
        take(sbuf.at[k], s_recv.at[k], NCOL - 1)
        sbuf[k, c] = ssrc[k]
        both = jnp.sum(sbuf[k], axis=0)
        return both[0:1, :], both[4:5, :]

    def apply(vec):
        out = matvec(xinv, vec)
        for _ in range(REFINE):
            out = out + matvec(xinv, vec - matvec(pmat, out))
        return out

    def spread_out(it, vec):
        zsrc[it] = vec
        each(1, NCOL, lambda d: zr_copy(it, d).start())
        each(1, NROW, lambda d: zc_copy(it, d).start())
        zbuf[it, ap] = vec
        zbuf[it, 2] = vec

    def products(it):
        for slot in range(3):
            @pl.when(not_p if slot == 2 else c != GR * r + slot)
            def _():
                z_from(it, slot).wait_recv()

        zc = zbuf[it, 2]
        back = [jnp.zeros((1, hi - lo), F32) for lo, hi in map(lanes, range(LT))]
        for a in range(GR):
            acc[a] = -spread(tile[a], zc)
            zcol = columns(zbuf[it, a])
            for t in range(LT):
                lo, hi = lanes(t)
                back[t] = back[t] + jnp.sum(tile[a, :, lo:hi] * zcol[:BLK, :hi - lo], axis=0, keepdims=True)
        rows = pl.ds(pl.multiple_of(part * CH, 8), CH)
        acc[half, rows, :] += spread(dchunk[...], zbuf[it, half])
        back[LT - 1] = jnp.concatenate([back[LT - 1], jnp.zeros((1, 128 * LT - BLK), F32)], axis=1)
        bsrc[it] = jnp.concatenate(back + [jnp.zeros((8 - LT, 128), F32)], axis=0)

        @pl.when(not_p)
        def _():
            b_copy(it).start()
        for a in range(GR):
            csrc[it, a] = fold(acc[a])

            @pl.when(c != GR * r + a)
            def _():
                c_copy(it, a).start()

    def collect(it):
        take(cbuf.at[it], c_recv.at[it], NCOL - 1)
        take(bbuf.at[it], b_recv.at[it], NROW - 1)
        cbuf[it, c] = csrc[it, ap]
        bbuf[it, r] = bsrc[it]
        return jnp.sum(cbuf[it], axis=0) - jnp.sum(bbuf[it], axis=0)

    @pl.when(is_p)
    def _():
        spread_out(0, apply(rhs[ap]))
    g_own = pltpu.make_async_copy(terms, gathered.at[c], g_loc)
    g_own.start()
    each(1, SIDE, lambda d: g_copy(d).start())
    products(0)
    pl.when(is_p)(pass_on)

    @pl.when(is_p)
    def _():
        image = collect(0)
        state[0] = image
        spread_out(1, apply(image))
        exchange(0, rhs[ap] * zsrc[0], zsrc[0] * image)
    products(1)

    pl.when(not_p)(pass_on)

    @pl.when(is_p)
    def _():
        first, image = zsrc[0], state[0]
        rz, curve = totals(0)
        alpha = rz / curve
        res = rhs[ap] - alpha * image
        second = first - alpha * zsrc[1]
        exchange(1, res * second, res * second)
        moved = image - alpha * collect(1)
        rz_next, _ = totals(1)
        beta = rz_next / rz
        direction = second + beta * first
        image = moved + beta * image
        exchange(2, direction * image, direction * image)
        curve, _ = totals(2)
        step = rz_next / curve
        fsrc[0] = alpha * first + step * direction
        fsrc[1] = res - step * image
        each(1, NCOL, lambda d: f_copy(d).start())
        fbuf[ap] = fsrc[...]

    for a in range(GR):
        @pl.when(c != GR * r + a)
        def _():
            f_from(a).wait_recv()
        sol[a] = fbuf[a, 0]
        resid[a] = fbuf[a, 1]
    each(1, SIDE, lambda d: g_last(d).wait_recv())
    each(1, SIDE, lambda d: g_copy(d).wait_send())
    each(1, SIDE, lambda d: g_second(d).wait_send())

    for it in range(ITERS):
        @pl.when(not_p)
        def _():
            b_copy(it).wait_send()
        for a in range(GR):
            @pl.when(c != GR * r + a)
            def _():
                c_copy(it, a).wait_send()

    @pl.when(is_p)
    def _():
        for it in range(ITERS):
            each(1, NCOL, lambda d: zr_copy(it, d).wait_send())
            each(1, NROW, lambda d: zc_copy(it, d).wait_send())
        for k in range(3):
            each(1, NCOL, lambda d: s_copy(k, d).wait_send())
        each(1, NCOL, lambda d: f_copy(d).wait_send())


def gradients(tile, dchunk, xinv, pmat, rhs, terms):
    vm = pl.BlockSpec(memory_space=pltpu.VMEM)
    dma = pltpu.SemaphoreType.DMA
    v = lambda *lead: pltpu.VMEM((*lead, 8, 128), F32)
    vec = jax.ShapeDtypeStruct((GR, 8, 128), F32)
    any_ = pl.BlockSpec(memory_space=pl.ANY)
    return pl.pallas_call(
        cg_kernel,
        out_shape=(jax.ShapeDtypeStruct((NCOL, CH, WIDE), BF16), vec, vec),
        in_specs=[any_, vm, any_, any_, vm, vm],
        out_specs=(any_, vm, vm),
        scratch_shapes=[
            pltpu.VMEM((GR, BLK, BLK), F32), pltpu.VMEM((BLK, BLK), F32), pltpu.VMEM((BLK, BLK), F32),
            v(ITERS, 3), v(ITERS), v(ITERS, NCOL), v(ITERS, GR), v(ITERS, NROW), v(ITERS), v(3, NCOL), v(3),
            v(GR, 2), v(2), pltpu.VMEM((GR, BLK, 128), F32), v(1),
            dma((3,)), dma, dma((2, SIDE)), dma((2, SIDE)), dma((ITERS, NCOL)), dma((ITERS, NROW)), dma((ITERS, 3)),
            dma((ITERS, GR)), dma((ITERS,)), dma((ITERS,)), dma((ITERS,)),
            dma((3, NCOL)), dma((3,)), dma((NCOL,)), dma((GR,)),
        ],
        compiler_params=pltpu.CompilerParams(collective_id=1, has_side_effects=True, vmem_limit_bytes=60 * 2**20),
        name="gradients",
    )(tile, dchunk, xinv, pmat, rhs, terms)


def subtract_kernel(cam, terms, out):
    rows = lax.broadcasted_iota(jnp.int32, (CH, BLK), 0)
    cols = lax.broadcasted_iota(jnp.int32, (CH, BLK), 1)
    for a in range(GR):
        for lo in range(0, BLK, CH):
            part = terms[a, lo:lo + CH, :]
            rest = part[:, BLK:BLK + 1].astype(F32)
            out[a, lo:lo + CH, :] = cam[a, lo:lo + CH, :] - (
                part[:, :BLK].astype(F32) + jnp.where(rows + lo == cols, rest, 0.0))


def subtract(cam, terms):
    vm = pl.BlockSpec(memory_space=pltpu.VMEM)
    return pl.pallas_call(
        subtract_kernel,
        out_shape=jax.ShapeDtypeStruct((GR, BLK, BLK), F32),
        in_specs=[vm, vm],
        out_specs=vm,
        compiler_params=pltpu.CompilerParams(vmem_limit_bytes=24 * 2**20),
        name="subtract",
    )(cam, terms)


def body(jac_row, jac_col, point_inv, pair_counts, camera_blocks, right_side):
    tile, dchunk, terms, pg = form(minv_table(point_inv, pair_counts), stack_rows(jac_row), stack_rows(jac_col),
                                   camera_blocks.reshape(NCOL, CH, BLK))
    xinv, pmat, pairs = inverse(pg.reshape(BLK, BLK), tile)
    wide = 128 * LT
    rhs = jnp.pad(right_side, ((0, 0), (0, wide - BLK))).reshape(GR, LT, 128)
    rhs = jnp.pad(rhs, ((0, 0), (0, 8 - LT), (0, 0)))
    gathered, sol, res = gradients(tile, dchunk, xinv, pmat, rhs, terms)
    diag = subtract(camera_blocks, gathered.reshape(GR, BLK, WIDE))
    back = lambda v: v[:, :LT].reshape(GR, wide)[:, :BLK]
    return pairs[:, None], diag, back(sol), back(res)


def solution(mesh):
    return jax.shard_map(
        body,
        mesh=mesh,
        in_specs=(
            P("row", "col", None, None, None, None, None),
            P("row", "col", None, None, None, None, None),
            P("row", "col", None, None, None, None),
            P("row", "col", None, None),
            P("row", None, None),
            P("row", None),
        ),
        out_specs=(
            P("row", "col", None, None),
            P("row", None, None),
            P("row", None),
            P("row", None),
        ),
        check_vma=False,
    )
```
